512 devices in a mesh: dp: 16 (over x, z_hi, core), dap: 32 (over y, z_lo).
Axes of the slice: x: 4, y: 4, z: 16 (z_hi: 2, z_lo: 8; z = z_hi * 8 + z_lo), core: 2. Of those that a mesh axis runs over, the one named last changes fastest.
Arguments:
- pair_repr: bfloat16 [16, 128, 128, 128], P('dp', 'dap'), may hold values from -16 to 16
- pair_mask: int32 [16, 128, 128], P('dp', 'dap'), may hold values from 0 to 1, as said below
- cotangent: bfloat16 [16, 128, 128, 128], P('dp', 'dap'), may hold values from -6 to 6
- proj_weight: bfloat16 [2, 128, 640], replicated, may hold values from -0.5 to 0.5
- proj_bias: float32 [2, 640], replicated, may hold values from -3 to 3
- norm_gain: float32 [2, 256], replicated, may hold values from 0.1 to 1.9
- norm_shift: float32 [2, 256], replicated, may hold values from -3 to 3
- out_weight: bfloat16 [2, 128, 128], replicated, may hold values from -0.5 to 0.5
- out_bias: float32 [2, 128], replicated, may hold values from -3 to 3
Outputs:
- pair_grad: bfloat16 [16, 128, 128, 128], P('dp', 'dap')
- proj_weight_grad: float32 [2, 128, 640], replicated
- out_weight_grad: float32 [2, 128, 128], replicated
The draws below stay inside these ranges and needn't reach their ends.
Inputs may be any that keep to these rules, and one draw needn't show every extreme that they name: pair_mask[c, i, j] is 1 exactly when residues i and j both lie below crop c's length, which is at least 64 and below 128.
All inputs are finite; a program needn't handle non-finite values.
Results may differ from the reference program's by a relative error of at most 0.015.
Values may be sent and summed in bfloat16 or wider, within the bound.
A program may use at most 64 MiB of HBM per device.

```python
import math
import jax
import jax.numpy as jnp
from jax import lax

C = 128
CH = 128
N = 128
CROPS = 16


def draw_pair_repr(key, part):
    key = jax.random.fold_in(key, 5)
    key_base, key_scale = jax.random.split(key, 2)
    cell_scale = jnp.exp(jax.random.uniform(key_scale, (CROPS, N, N, 1), jnp.float32, math.log(0.5), math.log(4.0)))
    values = jnp.clip(jax.random.normal(key_base, (CROPS, N, N, C), jnp.float32), -4.0, 4.0) * cell_scale
    return values.astype(jnp.bfloat16)


def draw_pair_mask(key, part):
    key = jax.random.fold_in(key, 11)
    lengths = jax.random.randint(key, (CROPS,), N // 2, N)
    positions = jnp.arange(N, dtype=jnp.int32)
    residue_valid = positions[None, :] < lengths[:, None]
    both_valid = residue_valid[:, :, None] & residue_valid[:, None, :]
    return both_valid.astype(jnp.int32)


def block_levels(own_key, shape, shards, least, high):
    level = 1.0
    for position, parts in shards:
        draws = jax.random.uniform(jax.random.fold_in(jax.random.fold_in(own_key, 6), position), (parts,), jnp.float32, least / len(shards), high / len(shards))
        level = level * jnp.repeat(jnp.exp(draws), shape[position] // parts).reshape((-1,) + (1,) * (len(shape) - 1 - position))
    return level


def bell_draw(key, extent, width, reach, shards=(), held_as=jnp.bfloat16):
    array = width * jax.random.normal(key, extent, jnp.float32)
    if shards:
        array = array * block_levels(key, extent, shards, -0.22, 0.18)
    return jnp.clip(array, -reach, reach).astype(held_as)


def setup_inputs(seed: int = 0) -> dict:
    key_list = jax.random.split(jax.random.key(seed), 10)
    pair_repr = draw_pair_repr(jax.random.fold_in(key_list[9], 71), 0)
    pair_mask = draw_pair_mask(jax.random.fold_in(key_list[9], 71), 0)
    cotangent = bell_draw(key_list[2], (CROPS, N, N, C), 1.0, 6.0, ((0, 16), (1, 32)))
    proj_weight = bell_draw(key_list[3], (2, C, 4 * CH + C), C ** -0.5, 0.5)
    proj_bias = bell_draw(key_list[4], (2, 4 * CH + C), 0.5, 3.0, (), jnp.float32)
    norm_gain = jnp.clip(1.0 + 0.18 * jax.random.normal(key_list[5], (2, C + CH), jnp.float32), 0.1, 1.9)
    norm_shift = bell_draw(key_list[6], (2, C + CH), 0.5, 3.0, (), jnp.float32)
    out_weight = bell_draw(key_list[7], (2, CH, C), CH ** -0.5, 0.5)
    out_bias = bell_draw(key_list[8], (2, C), 0.5, 3.0, (), jnp.float32)
    return {"pair_repr": pair_repr, "pair_mask": pair_mask, "cotangent": cotangent, "proj_weight": proj_weight, "proj_bias": proj_bias, "norm_gain": norm_gain, "norm_shift": norm_shift, "out_weight": out_weight, "out_bias": out_bias}


NORM_EPSILON = 1e-05

def layer_norm(values, gain_vec, shift_vec, norm_axis):
    mean_value = lax.optimization_barrier(jnp.mean(values, axis=norm_axis, keepdims=True))
    centred = values - mean_value
    variance = lax.optimization_barrier(jnp.mean(centred * centred, axis=norm_axis, keepdims=True))
    return centred * lax.rsqrt(variance + NORM_EPSILON) * gain_vec + shift_vec

def norm_pullback(values, gain_vec, shift_vec, norm_axis, upstream):
    _, pull_back = jax.vjp(lambda inner_value: layer_norm(inner_value, gain_vec, shift_vec, norm_axis), values)
    return pull_back(upstream)[0]

def edge_pair(edge_pre, cell_mask):
    left_edge = jax.nn.sigmoid(edge_pre[1]) * edge_pre[0] * cell_mask
    right_edge = jax.nn.sigmoid(edge_pre[3]) * edge_pre[2] * cell_mask
    return jnp.stack([left_edge, right_edge]).astype(jnp.bfloat16)

def edge_pullback(edge_pre, cell_mask, grad_pair):
    sig_left = jax.nn.sigmoid(edge_pre[1])
    sig_right = jax.nn.sigmoid(edge_pre[3])
    grad_left = grad_pair[0].astype(jnp.float32) * cell_mask
    grad_right = grad_pair[1].astype(jnp.float32) * cell_mask
    return jnp.stack([grad_left * sig_left, grad_left * edge_pre[0] * sig_left * (1.0 - sig_left), grad_right * sig_right, grad_right * edge_pre[2] * sig_right * (1.0 - sig_right)]).astype(jnp.bfloat16)

def triangle(pair_edges, outgoing):
    left_edge = pair_edges[0].astype(jnp.float32)
    right_edge = pair_edges[1].astype(jnp.float32)
    if outgoing:
        return jnp.einsum('cik,cjk->cij', left_edge, right_edge).astype(jnp.bfloat16)
    return jnp.einsum('cki,ckj->cij', left_edge, right_edge).astype(jnp.bfloat16)

def triangle_pullback(pair_edges, grad_product, outgoing):
    left_edge = pair_edges[0].astype(jnp.float32)
    right_edge = pair_edges[1].astype(jnp.float32)
    grad_prod = grad_product.astype(jnp.float32)
    if outgoing:
        grad_left = jnp.einsum('cij,cjk->cik', grad_prod, right_edge)
        grad_right = jnp.einsum('cij,cik->cjk', grad_prod, left_edge)
    else:
        grad_left = jnp.einsum('ckj,cij->cki', right_edge, grad_prod)
        grad_right = jnp.einsum('cki,cij->ckj', left_edge, grad_prod)
    return jnp.stack([grad_left, grad_right]).astype(jnp.bfloat16)

def crop_pass(crop_pair, crop_mask, crop_cot, proj_weight, proj_bias, norm_gain, norm_shift, out_weight, out_bias):
    cell_mask = crop_mask.astype(jnp.float32)
    pair_state = crop_pair
    records = []
    for update in range(2):
        w_edge = proj_weight[update, :, :4 * CH].reshape(C, 4, CH).astype(jnp.float32)
        w_gate = proj_weight[update, :, 4 * CH:].astype(jnp.float32)
        state_f = pair_state.astype(jnp.float32)
        normed = layer_norm(state_f, norm_gain[update, :C], norm_shift[update, :C], -1).astype(jnp.bfloat16)
        normed_f = normed.astype(jnp.float32)
        edge_pre = jnp.einsum('rnc,cgh->ghrn', normed_f, w_edge) + proj_bias[update, :4 * CH].reshape(4, CH, 1, 1)
        gate_pre = jnp.einsum('rnc,cd->rnd', normed_f, w_gate) + proj_bias[update, 4 * CH:]
        pair_edges = edge_pair(edge_pre, cell_mask)
        product = triangle(pair_edges, update == 0)
        mixed_norm = layer_norm(product.astype(jnp.float32), norm_gain[update, C:][:, None, None], norm_shift[update, C:][:, None, None], 0).astype(jnp.bfloat16)
        branch = jnp.einsum('hrn,hd->rnd', mixed_norm.astype(jnp.float32), out_weight[update].astype(jnp.float32)) + out_bias[update]
        records.append((state_f, normed, edge_pre, gate_pre, pair_edges, product, mixed_norm, branch))
        pair_state = (state_f + jax.nn.sigmoid(gate_pre) * branch).astype(jnp.bfloat16)
    upstream = crop_cot.astype(jnp.float32)
    proj_grads = []
    out_grads = []
    for update in (1, 0):
        state_f, normed, edge_pre, gate_pre, pair_edges, product, mixed_norm, branch = records[update]
        w_edge = proj_weight[update, :, :4 * CH].reshape(C, 4, CH).astype(jnp.float32)
        w_gate = proj_weight[update, :, 4 * CH:].astype(jnp.float32)
        gate_value = jax.nn.sigmoid(gate_pre)
        grad_branch = (upstream * gate_value).astype(jnp.bfloat16)
        grad_gate = (upstream * branch * gate_value * (1.0 - gate_value)).astype(jnp.bfloat16)
        out_grad = jnp.einsum('hrn,rnd->hd', mixed_norm.astype(jnp.float32), grad_branch.astype(jnp.float32))
        grad_mixed = jnp.einsum('rnd,hd->hrn', grad_branch.astype(jnp.float32), out_weight[update].astype(jnp.float32))
        grad_product = norm_pullback(product.astype(jnp.float32), norm_gain[update, C:][:, None, None], norm_shift[update, C:][:, None, None], 0, grad_mixed).astype(jnp.bfloat16)
        grad_pair = triangle_pullback(pair_edges, grad_product, update == 0)
        grad_edge = edge_pullback(edge_pre, cell_mask, grad_pair).astype(jnp.float32)
        normed_f = normed.astype(jnp.float32)
        grad_gate_f = grad_gate.astype(jnp.float32)
        edge_grad = jnp.einsum('rnc,ghrn->cgh', normed_f, grad_edge).reshape(C, 4 * CH)
        gate_grad = jnp.einsum('rnc,rnd->cd', normed_f, grad_gate_f)
        grad_normed = jnp.einsum('ghrn,cgh->rnc', grad_edge, w_edge) + jnp.einsum('rnd,cd->rnc', grad_gate_f, w_gate)
        upstream = upstream + norm_pullback(state_f, norm_gain[update, :C], norm_shift[update, :C], -1, grad_normed)
        proj_grads.append(jnp.concatenate([edge_grad, gate_grad], axis=1))
        out_grads.append(out_grad)
    return (upstream.astype(jnp.bfloat16), jnp.stack(proj_grads[::-1]), jnp.stack(out_grads[::-1]))

def reference(pair_repr, pair_mask, cotangent, proj_weight, proj_bias, norm_gain, norm_shift, out_weight, out_bias):

    def one_crop(carry, crop_inputs):
        crop_pair, crop_mask, crop_cot = crop_inputs
        crop_grad, proj_part, out_part = crop_pass(crop_pair, crop_mask, crop_cot, proj_weight, proj_bias, norm_gain, norm_shift, out_weight, out_bias)
        return ((carry[0] + proj_part, carry[1] + out_part), crop_grad)
    start = (jnp.zeros((2, C, 4 * CH + C), jnp.float32), jnp.zeros((2, CH, C), jnp.float32))
    totals, pair_grad = lax.scan(one_crop, start, (pair_repr, pair_mask, cotangent))
    return (pair_grad, totals[0], totals[1])
```

```python
import jax
import jax.numpy as jnp
from jax import lax
from jax.experimental import pallas as pl
from jax.experimental.pallas import tpu as pltpu
from jax.sharding import PartitionSpec as P

NORM_EPSILON = 1e-05
MESH = pl.DeviceIdType.MESH


def reduce_kernel(part_ref, total_ref, plane_buf, z_send, z_buf, own_total, all_buf, sems):
    dp = lax.axis_index("dp")
    dap = lax.axis_index("dap")
    core, z_hi, x = dp % 2, (dp // 2) % 2, dp // 4
    y, z_lo = dap // 8, dap % 8
    member = (x * 4 + y) * 2 + core
    z = z_hi * 8 + z_lo

    def plane_device(j):
        return ((j // 8) * 4 + z_hi * 2 + j % 2, ((j // 2) % 4) * 8 + z_lo)

    def line_device(k):
        return (x * 4 + (k // 8) * 2 + core, y * 8 + k % 8)

    barrier = pltpu.get_barrier_semaphore()

    @pl.loop(1, 32)
    def _(k):
        pl.semaphore_signal(
            barrier, inc=1, device_id=plane_device((member + k) % 32), device_id_type=MESH
        )

    @pl.loop(1, 16)
    def _(k):
        pl.semaphore_signal(
            barrier, inc=1, device_id=line_device((z + k) % 16), device_id_type=MESH
        )

    pl.semaphore_wait(barrier, 46)

    def remote(source, target, step, device):
        return pltpu.make_async_remote_copy(
            src_ref=source,
            dst_ref=target,
            send_sem=sems.at[2 * step],
            recv_sem=sems.at[2 * step + 1],
            device_id=device,
            device_id_type=MESH,
        )

    @pl.loop(1, 32)
    def _(k):
        j = (member + k) % 32
        remote(part_ref.at[j], plane_buf.at[member], 0, plane_device(j)).start()

    pltpu.make_async_copy(part_ref.at[member], plane_buf.at[member], sems.at[1]).start()
    pltpu.make_async_copy(plane_buf, plane_buf, sems.at[1]).wait()
    z_send[...] = jnp.sum(plane_buf[...].astype(jnp.float32), axis=0).astype(jnp.bfloat16)

    @pl.loop(1, 16)
    def _(k):
        remote(z_send, z_buf.at[z], 1, line_device((z + k) % 16)).start()

    pltpu.make_async_copy(z_send, z_buf.at[z], sems.at[3]).start()
    pltpu.make_async_copy(z_buf, z_buf, sems.at[3]).wait()
    own_total[...] = jnp.sum(z_buf[...].astype(jnp.float32), axis=0).astype(jnp.bfloat16)

    @pl.loop(1, 32)
    def _(k):
        remote(own_total, all_buf.at[member], 2, plane_device((member + k) % 32)).start()

    pltpu.make_async_copy(own_total, all_buf.at[member], sems.at[5]).start()
    pltpu.make_async_copy(all_buf, all_buf, sems.at[5]).wait()
    total_ref[...] = all_buf[...].astype(jnp.float32)
    sent = plane_buf.at[pl.ds(0, 31)]
    pltpu.make_async_copy(sent, sent, sems.at[0]).wait()
    sent = z_buf.at[pl.ds(0, 15)]
    pltpu.make_async_copy(sent, sent, sems.at[2]).wait()
    sent = all_buf.at[pl.ds(0, 31)]
    pltpu.make_async_copy(sent, sent, sems.at[4]).wait()


def reduce_everywhere(part):
    rows = part.shape[1]
    return pl.pallas_call(
        reduce_kernel,
        out_shape=jax.ShapeDtypeStruct(part.shape, jnp.float32),
        in_specs=[pl.BlockSpec(memory_space=pltpu.VMEM)],
        out_specs=pl.BlockSpec(memory_space=pltpu.VMEM),
        scratch_shapes=[
            pltpu.VMEM((32, rows, 128), jnp.bfloat16),
            pltpu.VMEM((rows, 128), jnp.bfloat16),
            pltpu.VMEM((16, rows, 128), jnp.bfloat16),
            pltpu.VMEM((rows, 128), jnp.bfloat16),
            pltpu.VMEM((32, rows, 128), jnp.bfloat16),
            pltpu.SemaphoreType.DMA((6,)),
        ],
        compiler_params=pltpu.CompilerParams(
            collective_id=1, has_side_effects=True, vmem_limit_bytes=32 << 20
        ),
    )(part)


def layer_norm(values, gain_vec, shift_vec, norm_axis):
    mean_value = jnp.mean(values, axis=norm_axis, keepdims=True)
    centred = values - mean_value
    variance = jnp.mean(centred * centred, axis=norm_axis, keepdims=True)
    return centred * lax.rsqrt(variance + NORM_EPSILON) * gain_vec + shift_vec


def norm_pullback(values, gain_vec, shift_vec, norm_axis, upstream):
    _, pull_back = jax.vjp(
        lambda inner_value: layer_norm(inner_value, gain_vec, shift_vec, norm_axis), values
    )
    return pull_back(upstream)[0]


def edge_pair(edge_pre, cell_mask):
    left_edge = jax.nn.sigmoid(edge_pre[1]) * edge_pre[0] * cell_mask
    right_edge = jax.nn.sigmoid(edge_pre[3]) * edge_pre[2] * cell_mask
    return jnp.stack([left_edge, right_edge]).astype(jnp.bfloat16)


def edge_pullback(edge_pre, cell_mask, grad_pair):
    sig_left = jax.nn.sigmoid(edge_pre[1])
    sig_right = jax.nn.sigmoid(edge_pre[3])
    grad_left = grad_pair[0].astype(jnp.float32) * cell_mask
    grad_right = grad_pair[1].astype(jnp.float32) * cell_mask
    return jnp.stack(
        [
            grad_left * sig_left,
            grad_left * edge_pre[0] * sig_left * (1.0 - sig_left),
            grad_right * sig_right,
            grad_right * edge_pre[2] * sig_right * (1.0 - sig_right),
        ]
    ).astype(jnp.bfloat16)


def triangle(pair_edges, outgoing):
    if outgoing:
        einsum_form = "cik,cjk->cij"
    else:
        einsum_form = "cki,ckj->cij"
    return jnp.einsum(
        einsum_form, pair_edges[0], pair_edges[1], preferred_element_type=jnp.float32
    ).astype(jnp.bfloat16)


def triangle_pullback(pair_edges, grad_product, outgoing):
    left_edge = pair_edges[0]
    right_edge = pair_edges[1]
    if outgoing:
        grad_left = jnp.einsum(
            "cij,cjk->cik", grad_product, right_edge, preferred_element_type=jnp.float32
        )
        grad_right = jnp.einsum(
            "cij,cik->cjk", grad_product, left_edge, preferred_element_type=jnp.float32
        )
    else:
        grad_left = jnp.einsum(
            "ckj,cij->cki", right_edge, grad_product, preferred_element_type=jnp.float32
        )
        grad_right = jnp.einsum(
            "cki,cij->ckj", left_edge, grad_product, preferred_element_type=jnp.float32
        )
    return jnp.stack([grad_left, grad_right]).astype(jnp.bfloat16)


def update_weights(proj_weight, proj_bias, norm_gain, norm_shift, update, channels, hidden):
    w_edge = proj_weight[update, :, : 4 * hidden].reshape(channels, 4, hidden)
    w_gate = proj_weight[update, :, 4 * hidden :]
    bias_edge = proj_bias[update, : 4 * hidden].reshape(4, hidden, 1, 1)
    bias_gate = proj_bias[update, 4 * hidden :]
    gain_in = norm_gain[update, :channels]
    shift_in = norm_shift[update, :channels]
    gain_out = norm_gain[update, channels:][:, None, None]
    shift_out = norm_shift[update, channels:][:, None, None]
    return (w_edge, w_gate, bias_edge, bias_gate, gain_in, shift_in, gain_out, shift_out)


def shards(
    pair_repr,
    pair_mask,
    cotangent,
    proj_weight,
    proj_bias,
    norm_gain,
    norm_shift,
    out_weight,
    out_bias,
):
    channels = pair_repr.shape[3]
    hidden = out_weight.shape[1]
    pair_state = pair_repr[0]
    cell_mask = pair_mask[0].astype(jnp.float32)
    records = []
    for update in range(2):
        w_edge, w_gate, bias_edge, bias_gate, gain_in, shift_in, gain_out, shift_out = (
            update_weights(proj_weight, proj_bias, norm_gain, norm_shift, update, channels, hidden)
        )
        state_f = pair_state.astype(jnp.float32)
        normed = layer_norm(state_f, gain_in, shift_in, -1).astype(jnp.bfloat16)
        edge_pre = (
            jnp.einsum("rnc,cgh->ghrn", normed, w_edge, preferred_element_type=jnp.float32)
            + bias_edge
        )
        gate_pre = (
            jnp.einsum("rnc,cd->rnd", normed, w_gate, preferred_element_type=jnp.float32)
            + bias_gate
        )
        pair_edges = edge_pair(edge_pre, cell_mask)
        spread = lax.all_to_all(pair_edges, "dap", split_axis=1, concat_axis=2, tiled=True)
        product = lax.all_to_all(
            triangle(spread, update == 0), "dap", split_axis=1, concat_axis=0, tiled=True
        )
        mixed_norm = layer_norm(product.astype(jnp.float32), gain_out, shift_out, 0).astype(
            jnp.bfloat16
        )
        branch = (
            jnp.einsum(
                "hrn,hd->rnd", mixed_norm, out_weight[update], preferred_element_type=jnp.float32
            )
            + out_bias[update]
        )
        records.append(
            (state_f, normed, edge_pre, gate_pre, pair_edges, spread, product, mixed_norm, branch)
        )
        pair_state = (state_f + jax.nn.sigmoid(gate_pre) * branch).astype(jnp.bfloat16)
    upstream = cotangent[0].astype(jnp.float32)
    proj_grads = []
    out_grads = []
    for update in (1, 0):
        state_f, normed, edge_pre, gate_pre, pair_edges, spread, product, mixed_norm, branch = (
            records[update]
        )
        w_edge, w_gate, bias_edge, bias_gate, gain_in, shift_in, gain_out, shift_out = (
            update_weights(proj_weight, proj_bias, norm_gain, norm_shift, update, channels, hidden)
        )
        gate_value = jax.nn.sigmoid(gate_pre)
        grad_branch = (upstream * gate_value).astype(jnp.bfloat16)
        grad_gate = (upstream * branch * gate_value * (1.0 - gate_value)).astype(jnp.bfloat16)
        out_grad = jnp.einsum(
            "hrn,rnd->hd", mixed_norm, grad_branch, preferred_element_type=jnp.float32
        )
        grad_mixed = jnp.einsum(
            "rnd,hd->hrn", grad_branch, out_weight[update], preferred_element_type=jnp.float32
        )
        grad_product = norm_pullback(
            product.astype(jnp.float32), gain_out, shift_out, 0, grad_mixed
        ).astype(jnp.bfloat16)
        column_edges, column_stack = (
            lax.all_to_all(pair_edges, "dap", split_axis=1, concat_axis=2, tiled=True),
            lax.all_to_all(grad_product[None], "dap", split_axis=1, concat_axis=2, tiled=True),
        )
        column_grad = column_stack[0]
        grad_pair = lax.all_to_all(
            triangle_pullback(column_edges, column_grad, update == 0),
            "dap",
            split_axis=2,
            concat_axis=1,
            tiled=True,
        )
        grad_edge = edge_pullback(edge_pre, cell_mask, grad_pair)
        edge_grad = jnp.einsum(
            "rnc,ghrn->cgh", normed, grad_edge, preferred_element_type=jnp.float32
        ).reshape(channels, 4 * hidden)
        gate_grad = jnp.einsum("rnc,rnd->cd", normed, grad_gate, preferred_element_type=jnp.float32)
        grad_normed = jnp.einsum(
            "ghrn,cgh->rnc", grad_edge, w_edge, preferred_element_type=jnp.float32
        )
        grad_normed = grad_normed + jnp.einsum(
            "rnd,cd->rnc", grad_gate, w_gate, preferred_element_type=jnp.float32
        )
        upstream = upstream + norm_pullback(state_f, gain_in, shift_in, -1, grad_normed)
        proj_part = jnp.concatenate([edge_grad, gate_grad], axis=1)
        proj_grads.append(proj_part)
        out_grads.append(out_grad)
    proj_total = jnp.stack(proj_grads[::-1])
    out_total = jnp.stack(out_grads[::-1])
    part = jnp.concatenate([proj_total.reshape(1280, 128), out_total.reshape(256, 128)])
    total = reduce_everywhere(part.astype(jnp.bfloat16).reshape(32, 48, 128)).reshape(1536, 128)
    proj_total = total[:1280].reshape(2, 128, 640)
    out_total = total[1280:].reshape(2, 128, 128)
    return (upstream.astype(jnp.bfloat16)[None], proj_total, out_total)


def solution(mesh):
    placed = (
        P("dp", "dap", None, None),
        P("dp", "dap", None),
        P("dp", "dap", None, None),
        P(),
        P(),
        P(),
        P(),
        P(),
        P(),
    )
    return jax.shard_map(
        shards,
        mesh=mesh,
        in_specs=placed,
        out_specs=(P("dp", "dap", None, None), P(), P()),
        check_vma=False,
    )
```

```python
import jax
import jax.numpy as jnp
from jax import lax
from jax.experimental import pallas as pl
from jax.experimental.pallas import tpu as pltpu
from jax.sharding import PartitionSpec as P

NORM_EPSILON = 1e-05
MESH = pl.DeviceIdType.MESH
F32 = jnp.float32
BF16 = jnp.bfloat16
EDGES, PRODUCTS, D_PRODUCTS, D_EDGES = 0, 2, 4, 6
GAIN_IN, SHIFT_IN, GAIN_OUT, SHIFT_OUT, OUT_BIAS = 5, 6, 7, 8, 9
TO_OWNER, FROM_OWNER, BY_CHANNEL, BY_SOURCE = 0, 1, 2, 3


def dot(a, b):
    return jnp.dot(a, b, preferred_element_type=F32)


def dot_nt(a, b):
    return lax.dot_general(a, b, (((1,), (1,)), ((), ())), preferred_element_type=F32)


def transposed(a):
    return a.astype(F32).T.astype(BF16)


def sigmoid(a):
    return 0.5 * jnp.tanh(0.5 * a) + 0.5


def channel_mean(a):
    return jnp.sum(a, axis=0, keepdims=True) * (1.0 / a.shape[0])


def normalise(values):
    centred = values - channel_mean(values)
    scale = lax.rsqrt(channel_mean(centred * centred) + NORM_EPSILON)
    return centred * scale, scale


def norm_pullback(unit, scale, d_unit):
    return scale * (d_unit - channel_mean(d_unit) - unit * channel_mean(d_unit * unit))


def each(count, body):
    for step in range(count):
        body(step)


def kernel(
    pair_ref,
    mask_ref,
    cot_ref,
    w_ref,
    bias_ref,
    gain_ref,
    shift_ref,
    wo_ref,
    ob_ref,
    grad_ref,
    proj_ref,
    out_ref,
    w_t,
    wo_t,
    perm,
    col,
    state,
    normed,
    unit_in,
    scale_in,
    edge,
    gate,
    branch,
    unit_out,
    scale_out,
    mixed,
    up,
    d_edge,
    d_branch,
    cm,
    own,
    own_out,
    edge_send,
    edge_recv,
    prod_send,
    prod_recv,
    dprod_send,
    dprod_recv,
    dedge_send,
    dedge_recv,
    sum_send,
    plane_buf,
    z_send,
    z_buf,
    own_total,
    all_buf,
    sems,
):
    dp = lax.axis_index("dp")
    dap = lax.axis_index("dap")
    core, z_hi, x = dp % 2, (dp // 2) % 2, dp // 4
    y, z_lo = dap // 8, dap % 8
    member = (x * 4 + y) * 2 + core
    z = z_hi * 8 + z_lo

    def plane_device(j):
        return ((j // 8) * 4 + z_hi * 2 + j % 2, ((j // 2) % 4) * 8 + z_lo)

    def line_device(k):
        return (x * 4 + (k // 8) * 2 + core, y * 8 + k % 8)

    def row_device(k):
        return (dp, k)

    barrier = pltpu.get_barrier_semaphore()

    def greet(device, own_index, count):
        @pl.loop(1, count)
        def _(k):
            pl.semaphore_signal(
                barrier, inc=1, device_id=device((own_index + k) % count), device_id_type=MESH
            )

    greet(row_device, dap, 32)
    greet(plane_device, member, 32)
    greet(line_device, z, 16)

    def send(source, target, step, device):
        pltpu.make_async_remote_copy(
            src_ref=source,
            dst_ref=target,
            send_sem=sems.at[2 * step],
            recv_sem=sems.at[2 * step + 1],
            device_id=device,
            device_id_type=MESH,
        ).start()

    def wait_bytes(ref, semaphore):
        pltpu.make_async_copy(ref, ref, sems.at[semaphore]).wait()

    def exchange(source, landing, u, step):
        @pl.loop(1, 32)
        def _(k):
            d = (dap + k) % 32
            send(source.at[u, d], landing.at[u, dap], step + u, row_device(d))

        pltpu.make_async_copy(
            source.at[u, dap], landing.at[u, dap], sems.at[2 * (step + u) + 1]
        ).start()

    def arrive(landing, u, step):
        wait_bytes(landing.at[u], 2 * (step + u) + 1)

    def prepare():
        row = lax.broadcasted_iota(jnp.int32, (128, 128), 0)
        lane = lax.broadcasted_iota(jnp.int32, (128, 128), 1)
        by_device = (row & 3) * 32 + (row >> 4) * 4 + ((row >> 2) & 3)
        by_device_t = (lane & 3) * 32 + (lane >> 4) * 4 + ((lane >> 2) & 3)
        by_channel = ((row >> 2) & 7) * 16 + (row >> 5) * 4 + (row & 3)
        by_channel_t = ((lane >> 2) & 7) * 16 + (lane >> 5) * 4 + (lane & 3)
        perm[TO_OWNER] = jnp.where(lane == by_device, 1.0, 0.0).astype(BF16)
        perm[FROM_OWNER] = jnp.where(row == by_device_t, 1.0, 0.0).astype(BF16)
        perm[BY_CHANNEL] = jnp.where(lane == by_channel, 1.0, 0.0).astype(BF16)
        perm[BY_SOURCE] = jnp.where(row == by_channel_t, 1.0, 0.0).astype(BF16)

    def prepare_update(u):
        rows = [bias_ref[u : u + 1, 128 * g : 128 * (g + 1)] for g in range(5)]
        rows += [gain_ref[u : u + 1, 0:128], shift_ref[u : u + 1, 0:128]]
        rows += [gain_ref[u : u + 1, 128:256], shift_ref[u : u + 1, 128:256]]
        rows += [ob_ref[u : u + 1, :]]
        for k, values in enumerate(rows):
            col[u, k] = jnp.broadcast_to(values, (128, 128)).T
        for g in range(5):
            block = slice(128 * g, 128 * (g + 1))
            w_t[u, block, :] = transposed(w_ref[u, :, block])
        wo_t[u] = transposed(wo_ref[u])

    def project(u, r):
        unit, scale = normalise(state[u, r])
        values = (unit * col[u, GAIN_IN] + col[u, SHIFT_IN]).astype(BF16)
        unit_in[u, r] = unit
        scale_in[u, r] = scale
        normed[u, r] = values
        keep = mask_ref[pl.ds(r, 1), :].astype(F32)
        for side in range(2):
            g = 2 * side
            pre = dot(w_t[u, 128 * g : 128 * (g + 2), :], values)
            linear = pre[:128] + col[u, g]
            opened = sigmoid(pre[128:] + col[u, g + 1])
            edge[u, r, g] = linear
            edge[u, r, g + 1] = opened
            cm[r, :, 128 * side : 128 * (side + 1)] = (opened * linear * keep).astype(BF16)

    def open_gate(u, r):
        gate[u, r] = sigmoid(dot(w_t[u, 512:640, :], normed[u, r]) + col[u, 4])

    def pack(target, u, g, values, width):
        block = slice(8 * g, 8 * (g + 1))
        for side in range(width):
            target[u, block, 16 * side : 16 * (side + 1), :] = values[
                :, 128 * side : 128 * (side + 1)
            ].reshape(8, 16, 128)

    def unpack(landing, u, g, width):
        block = slice(8 * g, 8 * (g + 1))
        sides = [
            landing[u, block, 16 * side : 16 * (side + 1), :].reshape(128, 128)
            for side in range(width)
        ]
        return sides[0] if width == 1 else jnp.concatenate(sides, axis=1)

    def to_messages(source, which, target, u, width):
        def group(g):
            rows = slice(32 * g, 32 * (g + 1))
            block = jnp.concatenate(
                [source[q, rows, 0 : 128 * width] for q in range(4)], axis=0
            )
            pack(target, u, g, dot(perm[which], block).astype(BF16), width)

        each(4, group)

    def from_messages(landing, which, u, target, width):
        def group(g):
            values = dot(perm[which], unpack(landing, u, g, width)).astype(BF16)
            for q in range(4):
                target(q, slice(32 * g, 32 * (g + 1)), values[32 * q : 32 * (q + 1)])

        each(4, group)

    def store_own(u):
        def store(q, rows, values):
            own[u, q, rows, :] = values

        return store

    def store_out(q, rows, values):
        own_out[q, rows, 0:128] = values

    def store_cm(width):
        def store(q, rows, values):
            cm[q, rows, 0 : 128 * width] = values

        return store

    def multiply(u, h):
        left, right = own[u, h, :, 0:128], own[u, h, :, 128:256]
        if u == 0:
            values = dot_nt(left, right)
        else:
            values = dot(transposed(left), right)
        own_out[h, :, 0:128] = values.astype(BF16)

    def multiply_back(u, h):
        left, right = own[u, h, :, 0:128], own[u, h, :, 128:256]
        d_product = own_out[h, :, 0:128]
        if u == 0:
            d_left = dot(d_product, right)
            d_right = dot(transposed(d_product), left)
        else:
            d_left = dot_nt(right, d_product)
            d_right = dot(left, d_product)
        own_out[h, :, 0:128] = d_left.astype(BF16)
        own_out[h, :, 128:256] = d_right.astype(BF16)

    def mix(u, r):
        unit, scale = normalise(cm[r, :, 0:128].astype(F32))
        values = (unit * col[u, GAIN_OUT] + col[u, SHIFT_OUT]).astype(BF16)
        unit_out[u, r] = unit
        scale_out[u, r] = scale
        mixed[u, r] = values
        result = dot(wo_t[u], values) + col[u, OUT_BIAS]
        branch[u, r] = result
        if u == 0:
            state[1, r] = (state[0, r] + gate[0, r] * result).astype(BF16).astype(F32)

    def forward(u):
        each(4, lambda r: project(u, r))
        to_messages(cm, TO_OWNER, edge_send, u, 2)
        if u == 0:
            pl.semaphore_wait(barrier, 77)
        exchange(edge_send, edge_recv, u, EDGES)
        each(4, lambda r: open_gate(u, r))
        if u == 0:
            prepare_update(1)

            def load_cotangent(r):
                up[r] = cot_ref[r].astype(F32).T

            each(4, load_cotangent)
        arrive(edge_recv, u, EDGES)
        from_messages(edge_recv, BY_CHANNEL, u, store_own(u), 2)
        each(4, lambda h: multiply(u, h))
        to_messages(own_out, BY_SOURCE, prod_send, u, 1)
        exchange(prod_send, prod_recv, u, PRODUCTS)
        arrive(prod_recv, u, PRODUCTS)
        from_messages(prod_recv, FROM_OWNER, u, store_cm(1), 1)
        each(4, lambda r: mix(u, r))

    def branch_back(u, r):
        opened = gate[u, r]
        through = up[r] * opened
        values = through.astype(BF16)
        d_branch[r] = values
        d_edge[r, 512:640, :] = (through * branch[u, r] * (1.0 - opened)).astype(BF16)
        d_unit = dot(wo_ref[u], values) * col[u, GAIN_OUT]
        cm[r, :, 0:128] = norm_pullback(unit_out[u, r], scale_out[u, r], d_unit).astype(BF16)

    def edges_back(u, r):
        keep = mask_ref[pl.ds(r, 1), :].astype(F32)
        for side in range(2):
            g = 2 * side
            linear, opened = edge[u, r, g], edge[u, r, g + 1]
            through = cm[r, :, 128 * side : 128 * (side + 1)].astype(F32) * keep * opened
            d_edge[r, 128 * g : 128 * (g + 1), :] = through.astype(BF16)
            d_edge[r, 128 * (g + 1) : 128 * (g + 2), :] = (
                through * linear * (1.0 - opened)
            ).astype(BF16)

    def norm_back(u, r):
        d_unit = dot(w_ref[u], d_edge[r]) * col[u, GAIN_IN]
        result = up[r] + norm_pullback(unit_in[u, r], scale_in[u, r], d_unit)
        if u == 1:
            up[r] = result
        else:
            grad_ref[r] = result.T.astype(BF16)

    def proj_part(u, g):
        total = dot_nt(normed[u, 0], d_edge[0, 128 * g : 128 * (g + 1), :])
        for r in range(1, 4):
            total += dot_nt(normed[u, r], d_edge[r, 128 * g : 128 * (g + 1), :])
        return total.astype(BF16).reshape(8, 16, 128)

    def out_part(u):
        total = dot_nt(mixed[u, 0], d_branch[0])
        for r in range(1, 4):
            total += dot_nt(mixed[u, r], d_branch[r])
        return total.astype(BF16).reshape(8, 16, 128)

    def sum_step(unit, stage):
        return 8 + 3 * unit + stage

    def sum_begin(unit):
        step = sum_step(unit, 0)

        @pl.loop(1, 32)
        def _(k):
            j = (member + k) % 32
            send(sum_send.at[unit, j], plane_buf.at[unit, member], step, plane_device(j))

        pltpu.make_async_copy(
            sum_send.at[unit, member], plane_buf.at[unit, member], sems.at[2 * step + 1]
        ).start()

    def sum_line(unit):
        wait_bytes(plane_buf.at[unit], 2 * sum_step(unit, 0) + 1)
        z_send[unit] = jnp.sum(plane_buf[unit].astype(F32), axis=0).astype(BF16)
        step = sum_step(unit, 1)

        @pl.loop(1, 16)
        def _(k):
            send(z_send.at[unit], z_buf.at[unit, z], step, line_device((z + k) % 16))

        pltpu.make_async_copy(
            z_send.at[unit], z_buf.at[unit, z], sems.at[2 * step + 1]
        ).start()

    def sum_share(unit):
        wait_bytes(z_buf.at[unit], 2 * sum_step(unit, 1) + 1)
        own_total[unit] = jnp.sum(z_buf[unit].astype(F32), axis=0).astype(BF16)
        step = sum_step(unit, 2)

        @pl.loop(1, 32)
        def _(k):
            send(
                own_total.at[unit],
                all_buf.at[unit, member],
                step,
                plane_device((member + k) % 32),
            )

        pltpu.make_async_copy(
            own_total.at[unit], all_buf.at[unit, member], sems.at[2 * step + 1]
        ).start()

    def sum_end(unit):
        wait_bytes(all_buf.at[unit], 2 * sum_step(unit, 2) + 1)
        for g in range(4):
            values = all_buf[unit, 8 * g : 8 * (g + 1)].reshape(128, 128).astype(F32)
            if unit == 1:
                u = 1 - g // 2
                if g % 2 == 0:
                    proj_ref[u, :, 512:640] = values
                else:
                    out_ref[u] = values
            else:
                proj_ref[1 - unit // 2, :, 128 * g : 128 * (g + 1)] = values

    def backward(u):
        each(4, lambda r: branch_back(u, r))
        to_messages(cm, TO_OWNER, dprod_send, u, 1)
        exchange(dprod_send, dprod_recv, u, D_PRODUCTS)
        first = 0 if u == 1 else 16
        sum_send[1, first : first + 8] = proj_part(u, 4)
        sum_send[1, first + 8 : first + 16] = out_part(u)
        if u == 0:
            sum_begin(1)
            sum_line(0)
        arrive(dprod_recv, u, D_PRODUCTS)
        from_messages(dprod_recv, BY_CHANNEL, u, store_out, 1)
        each(4, lambda h: multiply_back(u, h))
        to_messages(own_out, BY_SOURCE, dedge_send, u, 2)
        exchange(dedge_send, dedge_recv, u, D_EDGES)
        if u == 0:
            sum_share(0)
            sum_line(1)
        arrive(dedge_recv, u, D_EDGES)
        from_messages(dedge_recv, FROM_OWNER, u, store_cm(2), 2)
        each(4, lambda r: edges_back(u, r))
        unit = 0 if u == 1 else 2
        for g in range(4):
            sum_send[unit, 8 * g : 8 * (g + 1)] = proj_part(u, g)
        sum_begin(unit)
        each(4, lambda r: norm_back(u, r))

    prepare()
    prepare_update(0)

    def load_state(r):
        state[0, r] = pair_ref[r].astype(F32).T

    each(4, load_state)
    forward(0)
    forward(1)
    backward(1)
    backward(0)
    sum_share(1)
    sum_line(2)
    sum_end(0)
    sum_share(2)
    sum_end(1)
    sum_end(2)
    for step, sent in (
        (EDGES, edge_send),
        (PRODUCTS, prod_send),
        (D_PRODUCTS, dprod_send),
        (D_EDGES, dedge_send),
    ):
        for u in range(2):
            wait_bytes(sent.at[u, pl.ds(0, 31)], 2 * (step + u))
    for unit in range(3):
        wait_bytes(plane_buf.at[unit, pl.ds(0, 31)], 2 * sum_step(unit, 0))
        wait_bytes(z_buf.at[unit, pl.ds(0, 15)], 2 * sum_step(unit, 1))
        wait_bytes(all_buf.at[unit, pl.ds(0, 31)], 2 * sum_step(unit, 2))


def shards(
    pair_repr,
    pair_mask,
    cotangent,
    proj_weight,
    proj_bias,
    norm_gain,
    norm_shift,
    out_weight,
    out_bias,
):
    def real(*shape):
        return pltpu.VMEM(shape, F32)

    def half(*shape):
        return pltpu.VMEM(shape, BF16)

    vmem = pl.BlockSpec(memory_space=pltpu.VMEM)
    pair_grad, proj_grad, out_grad = pl.pallas_call(
        kernel,
        out_shape=(
            jax.ShapeDtypeStruct((4, 128, 128), BF16),
            jax.ShapeDtypeStruct((2, 128, 640), F32),
            jax.ShapeDtypeStruct((2, 128, 128), F32),
        ),
        in_specs=[vmem] * 9,
        out_specs=(vmem, vmem, vmem),
        scratch_shapes=[
            half(2, 640, 128),
            half(2, 128, 128),
            half(4, 128, 128),
            real(2, 10, 128, 128),
            real(2, 4, 128, 128),
            half(2, 4, 128, 128),
            real(2, 4, 128, 128),
            real(2, 4, 1, 128),
            real(2, 4, 4, 128, 128),
            real(2, 4, 128, 128),
            real(2, 4, 128, 128),
            real(2, 4, 128, 128),
            real(2, 4, 1, 128),
            half(2, 4, 128, 128),
            real(4, 128, 128),
            half(4, 640, 128),
            half(4, 128, 128),
            half(4, 128, 256),
            half(2, 4, 128, 256),
            half(4, 128, 256),
            half(2, 32, 32, 128),
            half(2, 32, 32, 128),
            half(2, 32, 16, 128),
            half(2, 32, 16, 128),
            half(2, 32, 16, 128),
            half(2, 32, 16, 128),
            half(2, 32, 32, 128),
            half(2, 32, 32, 128),
            half(3, 32, 16, 128),
            half(3, 32, 16, 128),
            half(3, 16, 128),
            half(3, 16, 16, 128),
            half(3, 16, 128),
            half(3, 32, 16, 128),
            pltpu.SemaphoreType.DMA((34,)),
        ],
        compiler_params=pltpu.CompilerParams(
            collective_id=1, has_side_effects=True, vmem_limit_bytes=40 << 20
        ),
    )(
        pair_repr[0],
        pair_mask[0],
        cotangent[0],
        proj_weight,
        proj_bias,
        norm_gain,
        norm_shift,
        out_weight,
        out_bias,
    )
    return pair_grad[None], proj_grad, out_grad


def solution(mesh):
    placed = (
        P("dp", "dap", None, None),
        P("dp", "dap", None),
        P("dp", "dap", None, None),
        P(),
        P(),
        P(),
        P(),
        P(),
        P(),
    )
    return jax.shard_map(
        shards,
        mesh=mesh,
        in_specs=placed,
        out_specs=(P("dp", "dap", None, None), P(), P()),
        check_vma=False,
    )
```

```python
import jax
import jax.numpy as jnp
from jax import lax
from jax.experimental import pallas as pl
from jax.experimental.pallas import tpu as pltpu
from jax.sharding import PartitionSpec as P

NORM_EPSILON = 1e-05
MESH = pl.DeviceIdType.MESH
F32 = jnp.float32
BF16 = jnp.bfloat16
EDGES, PRODUCTS, D_PRODUCTS, D_EDGES = 0, 2, 4, 6
GAIN_IN, SHIFT_IN, GAIN_OUT, SHIFT_OUT, OUT_BIAS = 5, 6, 7, 8, 9
TO_OWNER, FROM_OWNER, BY_CHANNEL, BY_SOURCE = 0, 1, 2, 3
LOADS, PAIR_SENT, PAIR_CAME, MASK_MOVE, COT_MOVE, GRAD_SENT, GRAD_CAME = 34, 40, 41, 45, 47, 49, 50


def dot(a, b):
    return jnp.dot(a, b, preferred_element_type=F32)


def dot_nt(a, b):
    return lax.dot_general(a, b, (((1,), (1,)), ((), ())), preferred_element_type=F32)


def transposed(a):
    return a.astype(F32).T.astype(BF16)


def sigmoid(a):
    return 0.5 * jnp.tanh(0.5 * a) + 0.5


def channel_mean(a):
    return jnp.sum(a, axis=0, keepdims=True) * (1.0 / a.shape[0])


def normalise(values):
    centred = values - channel_mean(values)
    scale = lax.rsqrt(channel_mean(centred * centred) + NORM_EPSILON)
    return centred * scale, scale


def norm_pullback(unit, scale, d_unit):
    return scale * (d_unit - channel_mean(d_unit) - unit * channel_mean(d_unit * unit))


def each(count, body):
    for step in range(count):
        body(step)


def kernel(
    pair_in,
    mask_in,
    cot_in,
    w_in,
    bias_in,
    gain_in,
    shift_in,
    wo_in,
    ob_in,
    grad_ref,
    proj_ref,
    out_ref,
    w_ref,
    bias_ref,
    gain_ref,
    shift_ref,
    wo_ref,
    ob_ref,
    mask_ref,
    pair_buf,
    cot_buf,
    grad_send,
    grad_buf,
    w_t,
    wo_t,
    perm,
    col,
    state,
    normed,
    unit_in,
    scale_in,
    edge,
    gate,
    branch,
    unit_out,
    scale_out,
    mixed,
    up,
    d_edge,
    d_branch,
    cm,
    own,
    own_out,
    edge_send,
    edge_recv,
    prod_send,
    prod_recv,
    dprod_send,
    dprod_recv,
    dedge_send,
    dedge_recv,
    sum_send,
    plane_buf,
    z_send,
    z_buf,
    own_total,
    all_buf,
    sems,
):
    dp = lax.axis_index("dp")
    dap = lax.axis_index("dap")
    core, z_hi, x = dp % 2, (dp // 2) % 2, dp // 4
    y, z_lo = dap // 8, dap % 8
    home_x = z_lo % 4
    member = y * 8 + core * 4 + x
    slot = y * 8 + core * 4 + (x + 4 - home_x) % 4
    z = z_hi * 8 + z_lo

    def member_device(k):
        return ((k % 4) * 4 + z_hi * 2 + (k // 4) % 2, (k // 8) * 8 + z_lo)

    def slot_device(k):
        return (((k + home_x) % 4) * 4 + z_hi * 2 + (k // 4) % 2, (k // 8) * 8 + z_lo)

    def line_device(k):
        return (x * 4 + (k // 8) * 2 + core, y * 8 + k % 8)

    worker = (((z_lo + x) % 4) * 4 + z_hi * 2 + z_lo // 4, y * 8 + core * 4 + x)
    home = (
        home_x * 4 + z_hi * 2 + z_lo // 4,
        slot,
    )
    away = (worker[0] != dp) | (worker[1] != dap)

    barrier = pltpu.get_barrier_semaphore()

    def greet(device, own_index, count):
        @pl.loop(1, count)
        def _(k):
            pl.semaphore_signal(
                barrier, inc=1, device_id=device((own_index + k) % count), device_id_type=MESH
            )

    @pl.when(away)
    def _():
        pl.semaphore_signal(barrier, inc=1, device_id=worker, device_id_type=MESH)
        pl.semaphore_signal(barrier, inc=1, device_id=home, device_id_type=MESH)

    greet(member_device, member, 32)
    greet(line_device, z, 16)

    def send(source, target, step, device):
        pltpu.make_async_remote_copy(
            src_ref=source,
            dst_ref=target,
            send_sem=sems.at[2 * step],
            recv_sem=sems.at[2 * step + 1],
            device_id=device,
            device_id_type=MESH,
        ).start()

    def wait_bytes(ref, semaphore):
        pltpu.make_async_copy(ref, ref, sems.at[semaphore]).wait()

    def far_first(k):
        order = 32 - k
        x_rank, y_rank = (order // 2) % 4, order // 8
        return (x_rank ^ (x_rank // 2)) + (order % 2) * 4 + (y_rank ^ (y_rank // 2)) * 8

    def exchange(source, landing, u, step):
        @pl.loop(1, 32)
        def _(k):
            d = slot ^ far_first(k)
            send(source.at[u, d], landing.at[u, slot], step + u, slot_device(d))

        pltpu.make_async_copy(
            source.at[u, slot], landing.at[u, slot], sems.at[2 * (step + u) + 1]
        ).start()

    def arrive(landing, u, step):
        wait_bytes(landing.at[u], 2 * (step + u) + 1)

    def move(source, target, sent, came, device):
        @pl.when(away)
        def _():
            pltpu.make_async_remote_copy(
                src_ref=source,
                dst_ref=target,
                send_sem=sems.at[sent],
                recv_sem=sems.at[came],
                device_id=device,
                device_id_type=MESH,
            ).start()

        @pl.when(jnp.logical_not(away))
        def _():
            pltpu.make_async_copy(source, target, sems.at[came]).start()

    def prepare():
        row = lax.broadcasted_iota(jnp.int32, (128, 128), 0)
        lane = lax.broadcasted_iota(jnp.int32, (128, 128), 1)
        by_device = (row & 3) * 32 + (row >> 4) * 4 + ((row >> 2) & 3)
        by_device_t = (lane & 3) * 32 + (lane >> 4) * 4 + ((lane >> 2) & 3)
        by_channel = ((row >> 2) & 7) * 16 + (row >> 5) * 4 + (row & 3)
        by_channel_t = ((lane >> 2) & 7) * 16 + (lane >> 5) * 4 + (lane & 3)
        perm[TO_OWNER] = jnp.where(lane == by_device, 1.0, 0.0).astype(BF16)
        perm[FROM_OWNER] = jnp.where(row == by_device_t, 1.0, 0.0).astype(BF16)
        perm[BY_CHANNEL] = jnp.where(lane == by_channel, 1.0, 0.0).astype(BF16)
        perm[BY_SOURCE] = jnp.where(row == by_channel_t, 1.0, 0.0).astype(BF16)

    def prepare_update(u):
        rows = [bias_ref[u : u + 1, 128 * g : 128 * (g + 1)] for g in range(5)]
        rows += [gain_ref[u : u + 1, 0:128], shift_ref[u : u + 1, 0:128]]
        rows += [gain_ref[u : u + 1, 128:256], shift_ref[u : u + 1, 128:256]]
        rows += [ob_ref[u : u + 1, :]]
        for k, values in enumerate(rows):
            col[u, k] = jnp.broadcast_to(values, (128, 128)).T
        for g in range(5):
            block = slice(128 * g, 128 * (g + 1))
            w_t[u, block, :] = transposed(w_ref[u, :, block])
        wo_t[u] = transposed(wo_ref[u])

    def project(u, r):
        unit, scale = normalise(state[u, r])
        values = (unit * col[u, GAIN_IN] + col[u, SHIFT_IN]).astype(BF16)
        unit_in[u, r] = unit
        scale_in[u, r] = scale
        normed[u, r] = values
        keep = mask_ref[pl.ds(r, 1), :].astype(F32)
        for side in range(2):
            g = 2 * side
            pre = dot(w_t[u, 128 * g : 128 * (g + 2), :], values)
            linear = pre[:128] + col[u, g]
            opened = sigmoid(pre[128:] + col[u, g + 1])
            edge[u, r, g] = linear
            edge[u, r, g + 1] = opened
            cm[r, :, 128 * side : 128 * (side + 1)] = (opened * linear * keep).astype(BF16)

    def open_gate(u, r):
        gate[u, r] = sigmoid(dot(w_t[u, 512:640, :], normed[u, r]) + col[u, 4])

    def pack(target, u, g, values, width):
        block = slice(8 * g, 8 * (g + 1))
        for side in range(width):
            target[u, block, 16 * side : 16 * (side + 1), :] = values[
                :, 128 * side : 128 * (side + 1)
            ].reshape(8, 16, 128)

    def unpack(landing, u, g, width):
        block = slice(8 * g, 8 * (g + 1))
        sides = [
            landing[u, block, 16 * side : 16 * (side + 1), :].reshape(128, 128)
            for side in range(width)
        ]
        return sides[0] if width == 1 else jnp.concatenate(sides, axis=1)

    def to_messages(source, which, target, u, width):
        def group(g):
            rows = slice(32 * g, 32 * (g + 1))
            block = jnp.concatenate(
                [source[q, rows, 0 : 128 * width] for q in range(4)], axis=0
            )
            pack(target, u, g, dot(perm[which], block).astype(BF16), width)

        each(4, group)

    def from_messages(landing, which, u, target, width):
        def group(g):
            values = dot(perm[which], unpack(landing, u, g, width)).astype(BF16)
            for q in range(4):
                target(q, slice(32 * g, 32 * (g + 1)), values[32 * q : 32 * (q + 1)])

        each(4, group)

    def store_own(u):
        def store(q, rows, values):
            own[u, q, rows, :] = values

        return store

    def store_out(q, rows, values):
        own_out[q, rows, 0:128] = values

    def store_cm(width):
        def store(q, rows, values):
            cm[q, rows, 0 : 128 * width] = values

        return store

    def multiply(u, h):
        left, right = own[u, h, :, 0:128], own[u, h, :, 128:256]
        if u == 0:
            values = dot_nt(left, right)
        else:
            values = dot(transposed(left), right)
        own_out[h, :, 0:128] = values.astype(BF16)

    def multiply_back(u, h):
        left, right = own[u, h, :, 0:128], own[u, h, :, 128:256]
        d_product = own_out[h, :, 0:128]
        if u == 0:
            d_left = dot(d_product, right)
            d_right = dot(transposed(d_product), left)
        else:
            d_left = dot_nt(right, d_product)
            d_right = dot(left, d_product)
        own_out[h, :, 0:128] = d_left.astype(BF16)
        own_out[h, :, 128:256] = d_right.astype(BF16)

    def mix(u, r):
        unit, scale = normalise(cm[r, :, 0:128].astype(F32))
        values = (unit * col[u, GAIN_OUT] + col[u, SHIFT_OUT]).astype(BF16)
        unit_out[u, r] = unit
        scale_out[u, r] = scale
        mixed[u, r] = values
        result = dot(wo_t[u], values) + col[u, OUT_BIAS]
        branch[u, r] = result
        if u == 0:
            state[1, r] = (state[0, r] + gate[0, r] * result).astype(BF16).astype(F32)

    def forward(u):
        if u == 0:
            for r in range(4):
                wait_bytes(pair_buf.at[r], PAIR_CAME + r)
                state[0, r] = pair_buf[r].astype(F32).T
                project(0, r)
        else:
            each(4, lambda r: project(u, r))
        to_messages(cm, TO_OWNER, edge_send, u, 2)
        exchange(edge_send, edge_recv, u, EDGES)
        each(4, lambda r: open_gate(u, r))
        if u == 0:
            move(cot_in, cot_buf, COT_MOVE, COT_MOVE + 1, worker)
        else:
            wait_bytes(cot_buf, COT_MOVE + 1)

            def load_cotangent(r):
                up[r] = cot_buf[r].astype(F32).T

            each(4, load_cotangent)
        arrive(edge_recv, u, EDGES)
        from_messages(edge_recv, BY_CHANNEL, u, store_own(u), 2)
        each(4, lambda h: multiply(u, h))
        to_messages(own_out, BY_SOURCE, prod_send, u, 1)
        exchange(prod_send, prod_recv, u, PRODUCTS)
        arrive(prod_recv, u, PRODUCTS)
        from_messages(prod_recv, FROM_OWNER, u, store_cm(1), 1)
        each(4, lambda r: mix(u, r))

    def branch_back(u, r):
        opened = gate[u, r]
        through = up[r] * opened
        values = through.astype(BF16)
        d_branch[r] = values
        d_edge[r, 512:640, :] = (through * branch[u, r] * (1.0 - opened)).astype(BF16)
        d_unit = dot(wo_ref[u], values) * col[u, GAIN_OUT]
        cm[r, :, 0:128] = norm_pullback(unit_out[u, r], scale_out[u, r], d_unit).astype(BF16)

    def edges_back(u, r):
        keep = mask_ref[pl.ds(r, 1), :].astype(F32)
        for side in range(2):
            g = 2 * side
            linear, opened = edge[u, r, g], edge[u, r, g + 1]
            through = cm[r, :, 128 * side : 128 * (side + 1)].astype(F32) * keep * opened
            d_edge[r, 128 * g : 128 * (g + 1), :] = through.astype(BF16)
            d_edge[r, 128 * (g + 1) : 128 * (g + 2), :] = (
                through * linear * (1.0 - opened)
            ).astype(BF16)

    def norm_back(u, r):
        d_unit = dot(w_ref[u], d_edge[r]) * col[u, GAIN_IN]
        result = up[r] + norm_pullback(unit_in[u, r], scale_in[u, r], d_unit)
        if u == 1:
            up[r] = result
        else:
            grad_send[r] = result.T.astype(BF16)
            move(grad_send.at[r], grad_buf.at[r], GRAD_SENT, GRAD_CAME, home)

    def proj_part(u, g):
        total = dot_nt(normed[u, 0], d_edge[0, 128 * g : 128 * (g + 1), :])
        for r in range(1, 4):
            total += dot_nt(normed[u, r], d_edge[r, 128 * g : 128 * (g + 1), :])
        return total.astype(BF16).reshape(8, 16, 128)

    def out_part(u):
        total = dot_nt(mixed[u, 0], d_branch[0])
        for r in range(1, 4):
            total += dot_nt(mixed[u, r], d_branch[r])
        return total.astype(BF16).reshape(8, 16, 128)

    def sum_step(unit, stage):
        return 8 + 3 * unit + stage

    def sum_begin(unit):
        step = sum_step(unit, 0)

        @pl.loop(1, 32)
        def _(k):
            j = member ^ far_first(k)
            send(sum_send.at[unit, j], plane_buf.at[unit, member], step, member_device(j))

        pltpu.make_async_copy(
            sum_send.at[unit, member], plane_buf.at[unit, member], sems.at[2 * step + 1]
        ).start()

    def sum_line(unit):
        wait_bytes(plane_buf.at[unit], 2 * sum_step(unit, 0) + 1)
        z_send[unit] = jnp.sum(plane_buf[unit].astype(F32), axis=0).astype(BF16)
        step = sum_step(unit, 1)

        @pl.loop(1, 16)
        def _(k):
            send(z_send.at[unit], z_buf.at[unit, z], step, line_device(z ^ k))

        pltpu.make_async_copy(
            z_send.at[unit], z_buf.at[unit, z], sems.at[2 * step + 1]
        ).start()

    def sum_share(unit):
        wait_bytes(z_buf.at[unit], 2 * sum_step(unit, 1) + 1)
        own_total[unit] = jnp.sum(z_buf[unit].astype(F32), axis=0).astype(BF16)
        step = sum_step(unit, 2)

        @pl.loop(1, 32)
        def _(k):
            send(
                own_total.at[unit],
                all_buf.at[unit, member],
                step,
                member_device(member ^ far_first(k)),
            )

        pltpu.make_async_copy(
            own_total.at[unit], all_buf.at[unit, member], sems.at[2 * step + 1]
        ).start()

    def sum_end(unit):
        wait_bytes(all_buf.at[unit], 2 * sum_step(unit, 2) + 1)
        for g in range(4):
            values = all_buf[unit, 8 * g : 8 * (g + 1)].reshape(128, 128).astype(F32)
            if unit == 1:
                u = 1 - g // 2
                if g % 2 == 0:
                    proj_ref[u, :, 512:640] = values
                else:
                    out_ref[u] = values
            else:
                proj_ref[1 - unit // 2, :, 128 * g : 128 * (g + 1)] = values

    def backward(u):
        each(4, lambda r: branch_back(u, r))
        to_messages(cm, TO_OWNER, dprod_send, u, 1)
        exchange(dprod_send, dprod_recv, u, D_PRODUCTS)
        first = 0 if u == 1 else 16
        sum_send[1, first : first + 8] = proj_part(u, 4)
        sum_send[1, first + 8 : first + 16] = out_part(u)
        if u == 0:
            sum_begin(1)
            sum_line(0)
        arrive(dprod_recv, u, D_PRODUCTS)
        from_messages(dprod_recv, BY_CHANNEL, u, store_out, 1)
        each(4, lambda h: multiply_back(u, h))
        to_messages(own_out, BY_SOURCE, dedge_send, u, 2)
        exchange(dedge_send, dedge_recv, u, D_EDGES)
        if u == 0:
            sum_share(0)
            sum_line(1)
        arrive(dedge_recv, u, D_EDGES)
        from_messages(dedge_recv, FROM_OWNER, u, store_cm(2), 2)
        each(4, lambda r: edges_back(u, r))
        unit = 0 if u == 1 else 2
        for g in range(4):
            sum_send[unit, 8 * g : 8 * (g + 1)] = proj_part(u, g)
        sum_begin(unit)
        each(4, lambda r: norm_back(u, r))

    loads = [
        pltpu.make_async_copy(source, target, sems.at[LOADS + k])
        for k, (source, target) in enumerate(
            (
                (w_in, w_ref),
                (bias_in, bias_ref),
                (gain_in, gain_ref),
                (shift_in, shift_ref),
                (wo_in, wo_ref),
                (ob_in, ob_ref),
            )
        )
    ]
    for load in loads:
        load.start()
    pl.semaphore_wait(barrier, jnp.where(away, 48, 46))

    move(mask_in, mask_ref, MASK_MOVE, MASK_MOVE + 1, worker)
    for r in range(4):
        move(pair_in.at[r], pair_buf.at[r], PAIR_SENT, PAIR_CAME + r, worker)
    for load in loads:
        load.wait()
    prepare()
    prepare_update(0)
    prepare_update(1)
    wait_bytes(mask_ref, MASK_MOVE + 1)
    forward(0)
    forward(1)
    backward(1)
    backward(0)
    sum_share(1)
    sum_line(2)
    sum_end(0)
    sum_share(2)
    sum_end(1)
    sum_end(2)
    wait_bytes(grad_buf, GRAD_CAME)
    grad_ref[...] = grad_buf[...]

    @pl.when(away)
    def _():
        wait_bytes(pair_buf, PAIR_SENT)
        wait_bytes(mask_ref, MASK_MOVE)
        wait_bytes(cot_buf, COT_MOVE)
        wait_bytes(grad_buf, GRAD_SENT)

    for step, sent in (
        (EDGES, edge_send),
        (PRODUCTS, prod_send),
        (D_PRODUCTS, dprod_send),
        (D_EDGES, dedge_send),
    ):
        for u in range(2):
            wait_bytes(sent.at[u, pl.ds(0, 31)], 2 * (step + u))
    for unit in range(3):
        wait_bytes(plane_buf.at[unit, pl.ds(0, 31)], 2 * sum_step(unit, 0))
        wait_bytes(z_buf.at[unit, pl.ds(0, 15)], 2 * sum_step(unit, 1))
        wait_bytes(all_buf.at[unit, pl.ds(0, 31)], 2 * sum_step(unit, 2))


def shards(
    pair_repr,
    pair_mask,
    cotangent,
    proj_weight,
    proj_bias,
    norm_gain,
    norm_shift,
    out_weight,
    out_bias,
):
    def real(*shape):
        return pltpu.VMEM(shape, F32)

    def half(*shape):
        return pltpu.VMEM(shape, BF16)

    vmem = pl.BlockSpec(memory_space=pltpu.VMEM)
    pair_grad, proj_grad, out_grad = pl.pallas_call(
        kernel,
        out_shape=(
            jax.ShapeDtypeStruct((4, 128, 128), BF16),
            jax.ShapeDtypeStruct((2, 128, 640), F32),
            jax.ShapeDtypeStruct((2, 128, 128), F32),
        ),
        in_specs=[pl.BlockSpec(memory_space=pl.ANY)] * 9,
        out_specs=(vmem, vmem, vmem),
        scratch_shapes=[
            half(2, 128, 640),
            real(2, 640),
            real(2, 256),
            real(2, 256),
            half(2, 128, 128),
            real(2, 128),
            pltpu.VMEM((4, 128), jnp.int32),
            half(4, 128, 128),
            half(4, 128, 128),
            half(4, 128, 128),
            half(4, 128, 128),
            half(2, 640, 128),
            half(2, 128, 128),
            half(4, 128, 128),
            real(2, 10, 128, 128),
            real(2, 4, 128, 128),
            half(2, 4, 128, 128),
            real(2, 4, 128, 128),
            real(2, 4, 1, 128),
            real(2, 4, 4, 128, 128),
            real(2, 4, 128, 128),
            real(2, 4, 128, 128),
            real(2, 4, 128, 128),
            real(2, 4, 1, 128),
            half(2, 4, 128, 128),
            real(4, 128, 128),
            half(4, 640, 128),
            half(4, 128, 128),
            half(4, 128, 256),
            half(2, 4, 128, 256),
            half(4, 128, 256),
            half(2, 32, 32, 128),
            half(2, 32, 32, 128),
            half(2, 32, 16, 128),
            half(2, 32, 16, 128),
            half(2, 32, 16, 128),
            half(2, 32, 16, 128),
            half(2, 32, 32, 128),
            half(2, 32, 32, 128),
            half(3, 32, 16, 128),
            half(3, 32, 16, 128),
            half(3, 16, 128),
            half(3, 16, 16, 128),
            half(3, 16, 128),
            half(3, 32, 16, 128),
            pltpu.SemaphoreType.DMA((51,)),
        ],
        compiler_params=pltpu.CompilerParams(
            collective_id=1, has_side_effects=True, vmem_limit_bytes=40 << 20
        ),
    )(
        pair_repr[0],
        pair_mask[0],
        cotangent[0],
        proj_weight,
        proj_bias,
        norm_gain,
        norm_shift,
        out_weight,
        out_bias,
    )
    return pair_grad[None], proj_grad, out_grad


def solution(mesh):
    placed = (
        P("dp", "dap", None, None),
        P("dp", "dap", None),
        P("dp", "dap", None, None),
        P(),
        P(),
        P(),
        P(),
        P(),
        P(),
    )
    return jax.shard_map(
        shards,
        mesh=mesh,
        in_specs=placed,
        out_specs=(P("dp", "dap", None, None), P(), P()),
        check_vma=False,
    )
```

```python
import jax
import jax.numpy as jnp
from jax import lax
from jax.experimental import pallas as pl
from jax.experimental.pallas import tpu as pltpu
from jax.sharding import PartitionSpec as P

NORM_EPSILON = 1e-05
MESH = pl.DeviceIdType.MESH
F32 = jnp.float32
BF16 = jnp.bfloat16
EDGES, PRODUCTS, D_PRODUCTS, D_EDGES = 0, 2, 4, 6
GAIN_IN, SHIFT_IN, GAIN_OUT, SHIFT_OUT, OUT_BIAS = 5, 6, 7, 8, 9
TO_OWNER, FROM_OWNER, BY_CHANNEL, BY_SOURCE = 0, 1, 2, 3
RECEIVED, EARLY, LATE, LOADS, PAIR_SENT, PAIR_CAME = 8, 40, 46, 52, 58, 59
MASK_MOVE, COT_MOVE, GRAD_SENT, GRAD_CAME, SEMAPHORES = 63, 65, 67, 68, 69
FAR_FIRST = (2, 3, 1, 0)


def dot(a, b):
    return jnp.dot(a, b, preferred_element_type=F32)


def dot_nt(a, b):
    return lax.dot_general(a, b, (((1,), (1,)), ((), ())), preferred_element_type=F32)


def transposed(a):
    return a.astype(F32).T.astype(BF16)


def sigmoid(a):
    return 0.5 * jnp.tanh(0.5 * a) + 0.5


def channel_mean(a):
    return jnp.sum(a, axis=0, keepdims=True) * (1.0 / a.shape[0])


def normalise(values):
    centred = values - channel_mean(values)
    scale = lax.rsqrt(channel_mean(centred * centred) + NORM_EPSILON)
    return centred * scale, scale


def norm_pullback(unit, scale, d_unit):
    return scale * (d_unit - channel_mean(d_unit) - unit * channel_mean(d_unit * unit))


def each(count, body):
    for step in range(count):
        body(step)


def kernel(
    pair_in,
    mask_in,
    cot_in,
    w_in,
    bias_in,
    gain_in,
    shift_in,
    wo_in,
    ob_in,
    grad_ref,
    proj_ref,
    out_ref,
    w_ref,
    bias_ref,
    gain_ref,
    shift_ref,
    wo_ref,
    ob_ref,
    mask_ref,
    pair_buf,
    cot_buf,
    grad_send,
    grad_buf,
    w_t,
    wo_t,
    perm,
    col,
    state,
    normed,
    unit_in,
    scale_in,
    edge,
    gate,
    branch,
    unit_out,
    scale_out,
    mixed,
    up,
    d_edge,
    d_branch,
    cm,
    own,
    own_out,
    edge_send,
    edge_recv,
    prod_send,
    prod_recv,
    dprod_send,
    dprod_recv,
    dedge_send,
    dedge_recv,
    early_part,
    early_planes,
    early_own,
    early_lines,
    early_sum,
    early_totals,
    late_part,
    late_planes,
    late_own,
    late_lines,
    late_sum,
    late_totals,
    sems,
):
    early = (early_part, early_planes, early_own, early_lines, early_sum, early_totals)
    late = (late_part, late_planes, late_own, late_lines, late_sum, late_totals)
    dp = lax.axis_index("dp")
    dap = lax.axis_index("dap")
    core, z_hi, x = dp & 1, (dp >> 1) & 1, dp >> 2
    y, z_lo = dap >> 3, dap & 7
    home_x = z_lo & 3
    member = y * 8 + core * 4 + x
    slot = y * 8 + core * 4 + ((x + 4 - home_x) & 3)
    z = z_hi * 8 + z_lo

    def member_device(k):
        return ((k & 3) * 4 + z_hi * 2 + ((k >> 2) & 1), (k >> 3) * 8 + z_lo)

    def slot_device(k):
        return (((k + home_x) & 3) * 4 + z_hi * 2 + ((k >> 2) & 1), (k >> 3) * 8 + z_lo)

    def line_device(k):
        return (x * 4 + (k >> 3) * 2 + core, y * 8 + (k & 7))

    worker = (((z_lo + x) & 3) * 4 + z_hi * 2 + (z_lo >> 2), y * 8 + core * 4 + x)
    home = (
        home_x * 4 + z_hi * 2 + (z_lo >> 2),
        slot,
    )
    away = (worker[0] != dp) | (worker[1] != dap)

    barrier = pltpu.get_barrier_semaphore()

    def greet(device, own_index, count):
        @pl.loop(1, count)
        def _(k):
            pl.semaphore_signal(
                barrier, inc=1, device_id=device((own_index + k) & (count - 1)), device_id_type=MESH
            )

    @pl.when(away)
    def _():
        pl.semaphore_signal(barrier, inc=1, device_id=worker, device_id_type=MESH)
        pl.semaphore_signal(barrier, inc=1, device_id=home, device_id_type=MESH)

    greet(member_device, member, 32)
    greet(line_device, z, 16)

    def send(source, target, sent, received, device):
        pltpu.make_async_remote_copy(
            src_ref=source,
            dst_ref=target,
            send_sem=sems.at[sent],
            recv_sem=sems.at[received],
            device_id=device,
            device_id_type=MESH,
        ).start()

    def wait_bytes(ref, semaphore):
        pltpu.make_async_copy(ref, ref, sems.at[semaphore]).wait()

    def far_first(k):
        order = 32 - k
        x_rank, y_rank = (order >> 1) & 3, order >> 3
        return (x_rank ^ (x_rank >> 1)) | ((order & 1) << 2) | ((y_rank ^ (y_rank >> 1)) << 3)

    def exchange_group(source, landing, u, step, apart):
        group = y ^ apart
        received = RECEIVED + 4 * (step + u) + y

        @pl.loop(0, 7 if apart == 0 else 8)
        def _(k):
            order = 7 - k
            x_rank = order >> 1
            offset = (x_rank ^ (x_rank >> 1)) | ((order & 1) << 2)
            d = group * 8 + ((slot & 7) ^ offset)
            send(
                source.at[u, d], landing.at[u, slot], step + u, received, slot_device(d)
            )

        if apart == 0:
            pltpu.make_async_copy(
                source.at[u, slot], landing.at[u, slot], sems.at[received]
            ).start()

    def move(source, target, sent, came, device):
        @pl.when(away)
        def _():
            pltpu.make_async_remote_copy(
                src_ref=source,
                dst_ref=target,
                send_sem=sems.at[sent],
                recv_sem=sems.at[came],
                device_id=device,
                device_id_type=MESH,
            ).start()

        @pl.when(jnp.logical_not(away))
        def _():
            pltpu.make_async_copy(source, target, sems.at[came]).start()

    def prepare():
        row = lax.broadcasted_iota(jnp.int32, (128, 128), 0)
        lane = lax.broadcasted_iota(jnp.int32, (128, 128), 1)
        by_device = (row & 3) * 32 + (row >> 4) * 4 + ((row >> 2) & 3)
        by_device_t = (lane & 3) * 32 + (lane >> 4) * 4 + ((lane >> 2) & 3)
        by_channel = ((row >> 2) & 7) * 16 + (row >> 5) * 4 + (row & 3)
        by_channel_t = ((lane >> 2) & 7) * 16 + (lane >> 5) * 4 + (lane & 3)
        perm[TO_OWNER] = jnp.where(lane == by_device, 1.0, 0.0).astype(BF16)
        perm[FROM_OWNER] = jnp.where(row == by_device_t, 1.0, 0.0).astype(BF16)
        perm[BY_CHANNEL] = jnp.where(lane == by_channel, 1.0, 0.0).astype(BF16)
        perm[BY_SOURCE] = jnp.where(row == by_channel_t, 1.0, 0.0).astype(BF16)

    def prepare_update(u):
        rows = [bias_ref[u : u + 1, 128 * g : 128 * (g + 1)] for g in range(5)]
        rows += [gain_ref[u : u + 1, 0:128], shift_ref[u : u + 1, 0:128]]
        rows += [gain_ref[u : u + 1, 128:256], shift_ref[u : u + 1, 128:256]]
        rows += [ob_ref[u : u + 1, :]]
        for k, values in enumerate(rows):
            col[u, k] = jnp.broadcast_to(values, (128, 128)).T
        for g in range(5):
            block = slice(128 * g, 128 * (g + 1))
            w_t[u, block, :] = transposed(w_ref[u, :, block])
        wo_t[u] = transposed(wo_ref[u])

    def project(u, r):
        unit, scale = normalise(state[u, r])
        values = (unit * col[u, GAIN_IN] + col[u, SHIFT_IN]).astype(BF16)
        unit_in[u, r] = unit
        scale_in[u, r] = scale
        normed[u, r] = values
        keep = mask_ref[pl.ds(r, 1), :].astype(F32)
        for side in range(2):
            g = 2 * side
            pre = dot(w_t[u, 128 * g : 128 * (g + 2), :], values)
            linear = pre[:128] + col[u, g]
            opened = sigmoid(pre[128:] + col[u, g + 1])
            edge[u, r, g] = linear
            edge[u, r, g + 1] = opened
            cm[r, :, 128 * side : 128 * (side + 1)] = (opened * linear * keep).astype(BF16)

    def open_gate(u, r):
        gate[u, r] = sigmoid(dot(w_t[u, 512:640, :], normed[u, r]) + col[u, 4])

    def pack(target, u, block, values, width):
        for side in range(width):
            target[u, block, 16 * side : 16 * (side + 1), :] = values[
                :, 128 * side : 128 * (side + 1)
            ].reshape(8, 16, 128)

    def unpack(landing, u, block, width):
        sides = [
            landing[u, block, 16 * side : 16 * (side + 1), :].reshape(128, 128)
            for side in range(width)
        ]
        return sides[0] if width == 1 else jnp.concatenate(sides, axis=1)

    def group_slices(apart):
        group = y ^ apart
        return (
            pl.ds(pl.multiple_of(group * 8, 8), 8),
            pl.ds(pl.multiple_of(group * 32, 32), 32),
        )

    def send_messages(source, which, target, landing, u, step, width):
        for apart in FAR_FIRST:
            block, rows = group_slices(apart)
            values = jnp.concatenate(
                [source[q, rows, 0 : 128 * width] for q in range(4)], axis=0
            )
            pack(target, u, block, dot(perm[which], values).astype(BF16), width)
            exchange_group(target, landing, u, step, apart)

    def take_messages(landing, which, u, step, target, width):
        for apart in FAR_FIRST:
            block, rows = group_slices(apart)
            wait_bytes(landing.at[u, block], RECEIVED + 4 * (step + u) + (y ^ apart))
            values = dot(perm[which], unpack(landing, u, block, width)).astype(BF16)
            for q in range(4):
                target(q, rows, values[32 * q : 32 * (q + 1)])

    def store_own(u):
        def store(q, rows, values):
            own[u, q, rows, :] = values

        return store

    def store_out(q, rows, values):
        own_out[q, rows, 0:128] = values

    def store_cm(width):
        def store(q, rows, values):
            cm[q, rows, 0 : 128 * width] = values

        return store

    def multiply(u, h):
        left, right = own[u, h, :, 0:128], own[u, h, :, 128:256]
        if u == 0:
            values = dot_nt(left, right)
        else:
            values = dot(transposed(left), right)
        own_out[h, :, 0:128] = values.astype(BF16)

    def multiply_back(u, h):
        left, right = own[u, h, :, 0:128], own[u, h, :, 128:256]
        d_product = own_out[h, :, 0:128]
        if u == 0:
            d_left = dot(d_product, right)
            d_right = dot(transposed(d_product), left)
        else:
            d_left = dot_nt(right, d_product)
            d_right = dot(left, d_product)
        own_out[h, :, 0:128] = d_left.astype(BF16)
        own_out[h, :, 128:256] = d_right.astype(BF16)

    def mix(u, r):
        unit, scale = normalise(cm[r, :, 0:128].astype(F32))
        values = (unit * col[u, GAIN_OUT] + col[u, SHIFT_OUT]).astype(BF16)
        unit_out[u, r] = unit
        scale_out[u, r] = scale
        mixed[u, r] = values
        result = dot(wo_t[u], values) + col[u, OUT_BIAS]
        branch[u, r] = result
        if u == 0:
            state[1, r] = (state[0, r] + gate[0, r] * result).astype(BF16).astype(F32)

    def forward(u):
        if u == 0:
            for r in range(4):
                wait_bytes(pair_buf.at[r], PAIR_CAME + r)
                state[0, r] = pair_buf[r].astype(F32).T
                project(0, r)
        else:
            each(4, lambda r: project(u, r))
        send_messages(cm, TO_OWNER, edge_send, edge_recv, u, EDGES, 2)
        each(4, lambda r: open_gate(u, r))
        if u == 0:
            move(cot_in, cot_buf, COT_MOVE, COT_MOVE + 1, worker)
        else:
            wait_bytes(cot_buf, COT_MOVE + 1)

            def load_cotangent(r):
                up[r] = cot_buf[r].astype(F32).T

            each(4, load_cotangent)
        take_messages(edge_recv, BY_CHANNEL, u, EDGES, store_own(u), 2)
        each(4, lambda h: multiply(u, h))
        send_messages(own_out, BY_SOURCE, prod_send, prod_recv, u, PRODUCTS, 1)
        take_messages(prod_recv, FROM_OWNER, u, PRODUCTS, store_cm(1), 1)
        each(4, lambda r: mix(u, r))

    def branch_back(u, r):
        opened = gate[u, r]
        through = up[r] * opened
        values = through.astype(BF16)
        d_branch[r] = values
        d_edge[r, 512:640, :] = (through * branch[u, r] * (1.0 - opened)).astype(BF16)
        d_unit = dot(wo_ref[u], values) * col[u, GAIN_OUT]
        cm[r, :, 0:128] = norm_pullback(unit_out[u, r], scale_out[u, r], d_unit).astype(BF16)

    def edges_back(u, r):
        keep = mask_ref[pl.ds(r, 1), :].astype(F32)
        for side in range(2):
            g = 2 * side
            linear, opened = edge[u, r, g], edge[u, r, g + 1]
            through = cm[r, :, 128 * side : 128 * (side + 1)].astype(F32) * keep * opened
            d_edge[r, 128 * g : 128 * (g + 1), :] = through.astype(BF16)
            d_edge[r, 128 * (g + 1) : 128 * (g + 2), :] = (
                through * linear * (1.0 - opened)
            ).astype(BF16)

    def norm_back(u, r):
        d_unit = dot(w_ref[u], d_edge[r]) * col[u, GAIN_IN]
        result = up[r] + norm_pullback(unit_in[u, r], scale_in[u, r], d_unit)
        if u == 1:
            up[r] = result
        else:
            grad_send[r] = result.T.astype(BF16)

    def send_grad(r):
        move(grad_send.at[r], grad_buf.at[r], GRAD_SENT, GRAD_CAME, home)

    def proj_part(u, g):
        total = dot_nt(normed[u, 0], d_edge[0, 128 * g : 128 * (g + 1), :])
        for r in range(1, 4):
            total += dot_nt(normed[u, r], d_edge[r, 128 * g : 128 * (g + 1), :])
        return total.astype(BF16)

    def out_part(u):
        total = dot_nt(mixed[u, 0], d_branch[0])
        for r in range(1, 4):
            total += dot_nt(mixed[u, r], d_branch[r])
        return total.astype(BF16)

    def begin_sum(unit, step):
        part, planes = unit[0], unit[1]

        @pl.loop(1, 32)
        def _(k):
            j = member ^ far_first(k)
            send(part.at[j], planes.at[member], step, step + 1, member_device(j))

        pltpu.make_async_copy(part.at[member], planes.at[member], sems.at[step + 1]).start()

    def sum_line(unit, step):
        planes, own_part, lines = unit[1], unit[2], unit[3]
        wait_bytes(planes, step + 1)
        own_part[...] = jnp.sum(planes[...].astype(F32), axis=0).astype(BF16)

        @pl.loop(1, 16)
        def _(k):
            send(own_part, lines.at[z], step + 2, step + 3, line_device(z ^ k))

        pltpu.make_async_copy(own_part, lines.at[z], sems.at[step + 3]).start()

    def share_sum(unit, step):
        lines, own_total, totals = unit[3], unit[4], unit[5]
        wait_bytes(lines, step + 3)
        own_total[...] = jnp.sum(lines[...].astype(F32), axis=0).astype(BF16)

        @pl.loop(1, 32)
        def _(k):
            send(
                own_total,
                totals.at[member],
                step + 4,
                step + 5,
                member_device(member ^ far_first(k)),
            )

        pltpu.make_async_copy(own_total, totals.at[member], sems.at[step + 5]).start()

    def sums_sent(unit, step):
        planes, lines, totals = unit[1], unit[3], unit[5]
        wait_bytes(planes.at[pl.ds(0, 31)], step)
        wait_bytes(lines.at[pl.ds(0, 15)], step + 2)
        wait_bytes(totals.at[pl.ds(0, 31)], step + 4)

    def put_early(block, values):
        early[0][4 * block : 4 * (block + 1)] = values.reshape(4, 32, 128)

    def end_early():
        wait_bytes(early[5], EARLY + 5)
        targets = [proj_ref.at[1, :, pl.ds(128 * g, 128)] for g in range(5)]
        targets += [out_ref.at[1], proj_ref.at[0, :, pl.ds(512, 128)], out_ref.at[0]]
        for block, target in enumerate(targets):
            values = early[5][4 * block : 4 * (block + 1)]
            target[...] = values.reshape(128, 128).astype(F32)

    def end_late():
        wait_bytes(late[5], LATE + 5)
        for g in range(4):
            values = late[5][8 * g : 8 * (g + 1)].reshape(128, 128)
            proj_ref[0, :, 128 * g : 128 * (g + 1)] = values.astype(F32)

    def backward(u):
        each(4, lambda r: branch_back(u, r))
        send_messages(cm, TO_OWNER, dprod_send, dprod_recv, u, D_PRODUCTS, 1)
        if u == 1:
            put_early(5, out_part(1))
            put_early(4, proj_part(1, 4))
        else:
            for g in range(4):
                put_early(g, proj_part(1, g))
            put_early(6, proj_part(0, 4))
            put_early(7, out_part(0))
            begin_sum(early, EARLY)
        take_messages(dprod_recv, BY_CHANNEL, u, D_PRODUCTS, store_out, 1)
        each(4, lambda h: multiply_back(u, h))
        send_messages(own_out, BY_SOURCE, dedge_send, dedge_recv, u, D_EDGES, 2)
        if u == 0:
            sum_line(early, EARLY)
        take_messages(dedge_recv, FROM_OWNER, u, D_EDGES, store_cm(2), 2)
        each(4, lambda r: edges_back(u, r))
        if u == 1:
            each(4, lambda r: norm_back(1, r))

    def finish():
        for g in range(4):
            values = proj_part(0, g)
            late[0][8 * g : 8 * (g + 1)] = values.reshape(8, 16, 128)
        begin_sum(late, LATE)
        for r in range(4):
            norm_back(0, r)
            if r < 2:
                send_grad(r)
        share_sum(early, EARLY)
        sum_line(late, LATE)
        send_grad(2)
        send_grad(3)
        end_early()
        share_sum(late, LATE)
        end_late()

    loads = [
        pltpu.make_async_copy(source, target, sems.at[LOADS + k])
        for k, (source, target) in enumerate(
            (
                (w_in, w_ref),
                (bias_in, bias_ref),
                (gain_in, gain_ref),
                (shift_in, shift_ref),
                (wo_in, wo_ref),
                (ob_in, ob_ref),
            )
        )
    ]
    for load in loads:
        load.start()
    pl.semaphore_wait(barrier, jnp.where(away, 48, 46))

    move(mask_in, mask_ref, MASK_MOVE, MASK_MOVE + 1, worker)
    for r in range(4):
        move(pair_in.at[r], pair_buf.at[r], PAIR_SENT, PAIR_CAME + r, worker)
    for load in loads:
        load.wait()
    prepare()
    prepare_update(0)
    prepare_update(1)
    wait_bytes(mask_ref, MASK_MOVE + 1)
    forward(0)
    forward(1)
    backward(1)
    backward(0)
    finish()
    wait_bytes(grad_buf, GRAD_CAME)
    grad_ref[...] = grad_buf[...]

    @pl.when(away)
    def _():
        wait_bytes(pair_buf, PAIR_SENT)
        wait_bytes(mask_ref, MASK_MOVE)
        wait_bytes(cot_buf, COT_MOVE)
        wait_bytes(grad_buf, GRAD_SENT)

    for step, sent in (
        (EDGES, edge_send),
        (PRODUCTS, prod_send),
        (D_PRODUCTS, dprod_send),
        (D_EDGES, dedge_send),
    ):
        for u in range(2):
            wait_bytes(sent.at[u, pl.ds(0, 31)], step + u)
    sums_sent(early, EARLY)
    sums_sent(late, LATE)


def shards(
    pair_repr,
    pair_mask,
    cotangent,
    proj_weight,
    proj_bias,
    norm_gain,
    norm_shift,
    out_weight,
    out_bias,
):
    def real(*shape):
        return pltpu.VMEM(shape, F32)

    def half(*shape):
        return pltpu.VMEM(shape, BF16)

    vmem = pl.BlockSpec(memory_space=pltpu.VMEM)
    pair_grad, proj_grad, out_grad = pl.pallas_call(
        kernel,
        out_shape=(
            jax.ShapeDtypeStruct((4, 128, 128), BF16),
            jax.ShapeDtypeStruct((2, 128, 640), F32),
            jax.ShapeDtypeStruct((2, 128, 128), F32),
        ),
        in_specs=[pl.BlockSpec(memory_space=pl.ANY)] * 9,
        out_specs=(vmem, vmem, vmem),
        scratch_shapes=[
            half(2, 128, 640),
            real(2, 640),
            real(2, 256),
            real(2, 256),
            half(2, 128, 128),
            real(2, 128),
            pltpu.VMEM((4, 128), jnp.int32),
            half(4, 128, 128),
            half(4, 128, 128),
            half(4, 128, 128),
            half(4, 128, 128),
            half(2, 640, 128),
            half(2, 128, 128),
            half(4, 128, 128),
            real(2, 10, 128, 128),
            real(2, 4, 128, 128),
            half(2, 4, 128, 128),
            real(2, 4, 128, 128),
            real(2, 4, 1, 128),
            real(2, 4, 4, 128, 128),
            real(2, 4, 128, 128),
            real(2, 4, 128, 128),
            real(2, 4, 128, 128),
            real(2, 4, 1, 128),
            half(2, 4, 128, 128),
            real(4, 128, 128),
            half(4, 640, 128),
            half(4, 128, 128),
            half(4, 128, 256),
            half(2, 4, 128, 256),
            half(4, 128, 256),
            half(2, 32, 32, 128),
            half(2, 32, 32, 128),
            half(2, 32, 16, 128),
            half(2, 32, 16, 128),
            half(2, 32, 16, 128),
            half(2, 32, 16, 128),
            half(2, 32, 32, 128),
            half(2, 32, 32, 128),
            half(32, 32, 128),
            half(32, 32, 128),
            half(32, 128),
            half(16, 32, 128),
            half(32, 128),
            half(32, 32, 128),
            half(32, 16, 128),
            half(32, 16, 128),
            half(16, 128),
            half(16, 16, 128),
            half(16, 128),
            half(32, 16, 128),
            pltpu.SemaphoreType.DMA((SEMAPHORES,)),
        ],
        compiler_params=pltpu.CompilerParams(
            collective_id=1, has_side_effects=True, vmem_limit_bytes=40 << 20
        ),
    )(
        pair_repr[0],
        pair_mask[0],
        cotangent[0],
        proj_weight,
        proj_bias,
        norm_gain,
        norm_shift,
        out_weight,
        out_bias,
    )
    return pair_grad[None], proj_grad, out_grad


def solution(mesh):
    placed = (
        P("dp", "dap", None, None),
        P("dp", "dap", None),
        P("dp", "dap", None, None),
        P(),
        P(),
        P(),
        P(),
        P(),
        P(),
    )
    return jax.shard_map(
        shards,
        mesh=mesh,
        in_specs=placed,
        out_specs=(P("dp", "dap", None, None), P(), P()),
        check_vma=False,
    )
```

```python
import jax
import jax.numpy as jnp
from jax import lax
from jax.experimental import pallas as pl
from jax.experimental.pallas import tpu as pltpu
from jax.sharding import PartitionSpec as P

NORM_EPSILON = 1e-05
MESH = pl.DeviceIdType.MESH
F32 = jnp.float32
BF16 = jnp.bfloat16
EDGES, PRODUCTS, D_PRODUCTS, D_EDGES = 0, 2, 4, 6
GAIN_IN, SHIFT_IN, GAIN_OUT, SHIFT_OUT, OUT_BIAS = 5, 6, 7, 8, 9
TO_OWNER, FROM_OWNER, BY_CHANNEL, BY_SOURCE = 0, 1, 2, 3
RECEIVED, EARLY, LATE, LOADS, PAIR_SENT, PAIR_CAME = 8, 40, 46, 52, 58, 59
MASK_MOVE, COT_MOVE, GRAD_SENT, GRAD_CAME, SEMAPHORES = 63, 65, 67, 68, 69
FAR_FIRST = (2, 3, 1, 0)


def dot(a, b):
    return jnp.dot(a, b, preferred_element_type=F32)


def dot_nt(a, b):
    return lax.dot_general(a, b, (((1,), (1,)), ((), ())), preferred_element_type=F32)


def transposed(a):
    return a.astype(F32).T.astype(BF16)


def sigmoid(a):
    return 0.5 * jnp.tanh(0.5 * a) + 0.5


def channel_mean(a):
    return jnp.sum(a, axis=0, keepdims=True) * (1.0 / a.shape[0])


def normalise(values):
    centred = values - channel_mean(values)
    scale = lax.rsqrt(channel_mean(centred * centred) + NORM_EPSILON)
    return centred * scale, scale


def norm_pullback(unit, scale, d_unit):
    return scale * (d_unit - channel_mean(d_unit) - unit * channel_mean(d_unit * unit))


def each(count, body):
    for step in range(count):
        body(step)


def kernel(
    pair_in,
    mask_in,
    cot_in,
    w_in,
    bias_in,
    gain_in,
    shift_in,
    wo_in,
    ob_in,
    grad_ref,
    proj_ref,
    out_ref,
    w_ref,
    bias_ref,
    gain_ref,
    shift_ref,
    wo_ref,
    ob_ref,
    mask_ref,
    pair_buf,
    cot_buf,
    grad_send,
    grad_buf,
    w_t,
    wo_t,
    perm,
    col,
    state,
    normed,
    unit_in,
    scale_in,
    edge,
    gate,
    branch,
    unit_out,
    scale_out,
    mixed,
    up,
    d_edge,
    d_branch,
    cm,
    own,
    own_out,
    edge_send,
    edge_recv,
    prod_send,
    prod_recv,
    dprod_send,
    dprod_recv,
    dedge_send,
    dedge_recv,
    early_part,
    early_planes,
    early_own,
    early_lines,
    early_sum,
    early_totals,
    late_part,
    late_planes,
    late_own,
    late_lines,
    late_sum,
    late_totals,
    sems,
):
    early = (early_part, early_planes, early_own, early_lines, early_sum, early_totals)
    late = (late_part, late_planes, late_own, late_lines, late_sum, late_totals)
    dp = lax.axis_index("dp")
    dap = lax.axis_index("dap")
    core, z_hi, x = dp & 1, (dp >> 1) & 1, dp >> 2
    y, z_lo = dap >> 3, dap & 7
    home_x = z_lo & 3
    member = y * 8 + core * 4 + x
    slot = y * 8 + core * 4 + ((x + 4 - home_x) & 3)
    z = z_hi * 8 + z_lo

    def member_device(k):
        return ((k & 3) * 4 + z_hi * 2 + ((k >> 2) & 1), (k >> 3) * 8 + z_lo)

    def slot_device(k):
        return (((k + home_x) & 3) * 4 + z_hi * 2 + ((k >> 2) & 1), (k >> 3) * 8 + z_lo)

    def line_device(k):
        return (x * 4 + (k >> 3) * 2 + core, y * 8 + (k & 7))

    worker = (((z_lo + x) & 3) * 4 + z_hi * 2 + (z_lo >> 2), y * 8 + core * 4 + x)
    home = (
        home_x * 4 + z_hi * 2 + (z_lo >> 2),
        slot,
    )
    away = (worker[0] != dp) | (worker[1] != dap)

    barrier = pltpu.get_barrier_semaphore()

    def greet(device, own_index, count):
        @pl.loop(1, count)
        def _(k):
            pl.semaphore_signal(
                barrier, inc=1, device_id=device((own_index + k) & (count - 1)), device_id_type=MESH
            )

    @pl.when(away)
    def _():
        pl.semaphore_signal(barrier, inc=1, device_id=worker, device_id_type=MESH)
        pl.semaphore_signal(barrier, inc=1, device_id=home, device_id_type=MESH)

    greet(member_device, member, 32)
    greet(line_device, z, 16)

    def send(source, target, sent, received, device):
        pltpu.make_async_remote_copy(
            src_ref=source,
            dst_ref=target,
            send_sem=sems.at[sent],
            recv_sem=sems.at[received],
            device_id=device,
            device_id_type=MESH,
        ).start()

    def wait_bytes(ref, semaphore):
        pltpu.make_async_copy(ref, ref, sems.at[semaphore]).wait()

    def far_first(k):
        order = 32 - k
        x_rank, y_rank = (order >> 1) & 3, order >> 3
        return (x_rank ^ (x_rank >> 1)) | ((order & 1) << 2) | ((y_rank ^ (y_rank >> 1)) << 3)

    def exchange_group(source, landing, u, step, apart):
        group = y ^ apart
        received = RECEIVED + 4 * (step + u) + y

        @pl.loop(0, 7 if apart == 0 else 8)
        def _(k):
            order = 7 - k
            x_rank = order >> 1
            offset = (x_rank ^ (x_rank >> 1)) | ((order & 1) << 2)
            d = group * 8 + ((slot & 7) ^ offset)
            send(
                source.at[u, d], landing.at[u, slot], step + u, received, slot_device(d)
            )

        if apart == 0:
            pltpu.make_async_copy(
                source.at[u, slot], landing.at[u, slot], sems.at[received]
            ).start()

    def move(source, target, sent, came, device):
        @pl.when(away)
        def _():
            pltpu.make_async_remote_copy(
                src_ref=source,
                dst_ref=target,
                send_sem=sems.at[sent],
                recv_sem=sems.at[came],
                device_id=device,
                device_id_type=MESH,
            ).start()

        @pl.when(jnp.logical_not(away))
        def _():
            pltpu.make_async_copy(source, target, sems.at[came]).start()

    def prepare():
        row = lax.broadcasted_iota(jnp.int32, (128, 128), 0)
        lane = lax.broadcasted_iota(jnp.int32, (128, 128), 1)
        by_device = (row & 3) * 32 + (row >> 4) * 4 + ((row >> 2) & 3)
        by_device_t = (lane & 3) * 32 + (lane >> 4) * 4 + ((lane >> 2) & 3)
        by_channel = ((row >> 2) & 7) * 16 + (row >> 5) * 4 + (row & 3)
        by_channel_t = ((lane >> 2) & 7) * 16 + (lane >> 5) * 4 + (lane & 3)
        perm[TO_OWNER] = jnp.where(lane == by_device, 1.0, 0.0).astype(BF16)
        perm[FROM_OWNER] = jnp.where(row == by_device_t, 1.0, 0.0).astype(BF16)
        perm[BY_CHANNEL] = jnp.where(lane == by_channel, 1.0, 0.0).astype(BF16)
        perm[BY_SOURCE] = jnp.where(row == by_channel_t, 1.0, 0.0).astype(BF16)

    def prepare_update(u):
        rows = [bias_ref[u : u + 1, 128 * g : 128 * (g + 1)] for g in range(5)]
        rows += [gain_ref[u : u + 1, 0:128], shift_ref[u : u + 1, 0:128]]
        rows += [gain_ref[u : u + 1, 128:256], shift_ref[u : u + 1, 128:256]]
        rows += [ob_ref[u : u + 1, :]]
        for k, values in enumerate(rows):
            col[u, k] = jnp.broadcast_to(values, (128, 128)).T
        for g in range(5):
            block = slice(128 * g, 128 * (g + 1))
            w_t[u, block, :] = transposed(w_ref[u, :, block])
        wo_t[u] = transposed(wo_ref[u])

    def project(u, r):
        unit, scale = normalise(state[u, r])
        values = (unit * col[u, GAIN_IN] + col[u, SHIFT_IN]).astype(BF16)
        unit_in[u, r] = unit
        scale_in[u, r] = scale
        normed[u, r] = values
        keep = mask_ref[pl.ds(r, 1), :].astype(F32)
        for side in range(2):
            g = 2 * side
            pre = dot(w_t[u, 128 * g : 128 * (g + 2), :], values)
            linear = pre[:128] + col[u, g]
            opened = sigmoid(pre[128:] + col[u, g + 1])
            edge[u, r, g] = linear
            edge[u, r, g + 1] = opened
            cm[r, :, 128 * side : 128 * (side + 1)] = (opened * linear * keep).astype(BF16)

    def open_gate(u, r):
        gate[u, r] = sigmoid(dot(w_t[u, 512:640, :], normed[u, r]) + col[u, 4])

    def pack(target, u, block, values, width):
        for side in range(width):
            target[u, block, 16 * side : 16 * (side + 1), :] = values[
                :, 128 * side : 128 * (side + 1)
            ].reshape(8, 16, 128)

    def unpack(landing, u, block, width):
        sides = [
            landing[u, block, 16 * side : 16 * (side + 1), :].reshape(128, 128)
            for side in range(width)
        ]
        return sides[0] if width == 1 else jnp.concatenate(sides, axis=1)

    def group_slices(apart):
        group = y ^ apart
        return (
            pl.ds(pl.multiple_of(group * 8, 8), 8),
            pl.ds(pl.multiple_of(group * 32, 32), 32),
        )

    def send_messages(source, which, target, landing, u, step, width):
        for apart in FAR_FIRST:
            block, rows = group_slices(apart)
            values = jnp.concatenate(
                [source[q, rows, 0 : 128 * width] for q in range(4)], axis=0
            )
            pack(target, u, block, dot(perm[which], values).astype(BF16), width)
            exchange_group(target, landing, u, step, apart)

    def take_messages(landing, which, u, step, target, width):
        for apart in FAR_FIRST:
            block, rows = group_slices(apart)
            wait_bytes(landing.at[u, block], RECEIVED + 4 * (step + u) + (y ^ apart))
            values = dot(perm[which], unpack(landing, u, block, width)).astype(BF16)
            for q in range(4):
                target(q, rows, values[32 * q : 32 * (q + 1)])

    def store_own(u):
        def store(q, rows, values):
            own[u, q, rows, :] = values

        return store

    def store_out(q, rows, values):
        own_out[q, rows, 0:128] = values

    def store_cm(width):
        def store(q, rows, values):
            cm[q, rows, 0 : 128 * width] = values

        return store

    def multiply(u, h):
        left, right = own[u, h, :, 0:128], own[u, h, :, 128:256]
        if u == 0:
            values = dot_nt(left, right)
        else:
            values = dot(transposed(left), right)
        own_out[h, :, 0:128] = values.astype(BF16)

    def multiply_back(u, h):
        left, right = own[u, h, :, 0:128], own[u, h, :, 128:256]
        d_product = own_out[h, :, 0:128]
        if u == 0:
            d_left = dot(d_product, right)
            d_right = dot(transposed(d_product), left)
        else:
            d_left = dot_nt(right, d_product)
            d_right = dot(left, d_product)
        own_out[h, :, 0:128] = d_left.astype(BF16)
        own_out[h, :, 128:256] = d_right.astype(BF16)

    def mix(u, r):
        unit, scale = normalise(cm[r, :, 0:128].astype(F32))
        values = (unit * col[u, GAIN_OUT] + col[u, SHIFT_OUT]).astype(BF16)
        unit_out[u, r] = unit
        scale_out[u, r] = scale
        mixed[u, r] = values
        result = dot(wo_t[u], values) + col[u, OUT_BIAS]
        branch[u, r] = result
        if u == 0:
            state[1, r] = (state[0, r] + gate[0, r] * result).astype(BF16).astype(F32)

    def forward(u):
        if u == 0:
            for r in range(4):
                wait_bytes(pair_buf.at[r], PAIR_CAME + r)
                state[0, r] = pair_buf[r].astype(F32).T
                project(0, r)
        else:
            each(4, lambda r: project(u, r))
        send_messages(cm, TO_OWNER, edge_send, edge_recv, u, EDGES, 2)
        each(4, lambda r: open_gate(u, r))
        if u == 0:
            move(cot_in, cot_buf, COT_MOVE, COT_MOVE + 1, worker)
        else:
            wait_bytes(cot_buf, COT_MOVE + 1)

            def load_cotangent(r):
                up[r] = cot_buf[r].astype(F32).T

            each(4, load_cotangent)
        take_messages(edge_recv, BY_CHANNEL, u, EDGES, store_own(u), 2)
        each(4, lambda h: multiply(u, h))
        send_messages(own_out, BY_SOURCE, prod_send, prod_recv, u, PRODUCTS, 1)
        take_messages(prod_recv, FROM_OWNER, u, PRODUCTS, store_cm(1), 1)
        each(4, lambda r: mix(u, r))

    def branch_back(u, r):
        opened = gate[u, r]
        through = up[r] * opened
        values = through.astype(BF16)
        d_branch[r] = values
        d_edge[r, 512:640, :] = (through * branch[u, r] * (1.0 - opened)).astype(BF16)
        d_unit = dot(wo_ref[u], values) * col[u, GAIN_OUT]
        cm[r, :, 0:128] = norm_pullback(unit_out[u, r], scale_out[u, r], d_unit).astype(BF16)

    def edges_back(u, r):
        keep = mask_ref[pl.ds(r, 1), :].astype(F32)
        for side in range(2):
            g = 2 * side
            linear, opened = edge[u, r, g], edge[u, r, g + 1]
            through = cm[r, :, 128 * side : 128 * (side + 1)].astype(F32) * keep * opened
            d_edge[r, 128 * g : 128 * (g + 1), :] = through.astype(BF16)
            d_edge[r, 128 * (g + 1) : 128 * (g + 2), :] = (
                through * linear * (1.0 - opened)
            ).astype(BF16)

    def norm_back(u, r):
        d_unit = dot(w_ref[u], d_edge[r]) * col[u, GAIN_IN]
        result = up[r] + norm_pullback(unit_in[u, r], scale_in[u, r], d_unit)
        if u == 1:
            up[r] = result
        else:
            grad_send[r] = result.T.astype(BF16)

    def send_grad(r):
        move(grad_send.at[r], grad_buf.at[r], GRAD_SENT, GRAD_CAME, home)

    def proj_part(u, g):
        total = dot_nt(normed[u, 0], d_edge[0, 128 * g : 128 * (g + 1), :])
        for r in range(1, 4):
            total += dot_nt(normed[u, r], d_edge[r, 128 * g : 128 * (g + 1), :])
        return total.astype(BF16)

    def out_part(u):
        total = dot_nt(mixed[u, 0], d_branch[0])
        for r in range(1, 4):
            total += dot_nt(mixed[u, r], d_branch[r])
        return total.astype(BF16)

    def begin_sum(unit, step):
        part, planes = unit[0], unit[1]

        @pl.loop(1, 32)
        def _(k):
            j = member ^ far_first(k)
            send(part.at[j], planes.at[member], step, step + 1, member_device(j))

        pltpu.make_async_copy(part.at[member], planes.at[member], sems.at[step + 1]).start()

    def sum_line(unit, step):
        planes, own_part, lines = unit[1], unit[2], unit[3]
        wait_bytes(planes, step + 1)
        own_part[...] = jnp.sum(planes[...].astype(F32), axis=0).astype(BF16)

        @pl.loop(1, 16)
        def _(k):
            send(own_part, lines.at[z], step + 2, step + 3, line_device(z ^ k))

        pltpu.make_async_copy(own_part, lines.at[z], sems.at[step + 3]).start()

    def share_sum(unit, step):
        lines, own_total, totals = unit[3], unit[4], unit[5]
        wait_bytes(lines, step + 3)
        own_total[...] = jnp.sum(lines[...].astype(F32), axis=0).astype(BF16)

        @pl.loop(1, 32)
        def _(k):
            send(
                own_total,
                totals.at[member],
                step + 4,
                step + 5,
                member_device(member ^ far_first(k)),
            )

        pltpu.make_async_copy(own_total, totals.at[member], sems.at[step + 5]).start()

    def sums_sent(unit, step):
        planes, lines, totals = unit[1], unit[3], unit[5]
        wait_bytes(planes.at[pl.ds(0, 31)], step)
        wait_bytes(lines.at[pl.ds(0, 15)], step + 2)
        wait_bytes(totals.at[pl.ds(0, 31)], step + 4)

    def put_early(block, values):
        early[0][4 * block : 4 * (block + 1)] = values.reshape(4, 32, 128)

    def end_early():
        wait_bytes(early[5], EARLY + 5)
        targets = [proj_ref.at[1, :, pl.ds(128 * g, 128)] for g in range(5)]
        targets += [out_ref.at[1], proj_ref.at[0, :, pl.ds(512, 128)], out_ref.at[0]]
        for block, target in enumerate(targets):
            values = early[5][4 * block : 4 * (block + 1)]
            target[...] = values.reshape(128, 128).astype(F32)

    def end_late():
        wait_bytes(late[5], LATE + 5)
        for g in range(4):
            values = late[5][8 * g : 8 * (g + 1)].reshape(128, 128)
            proj_ref[0, :, 128 * g : 128 * (g + 1)] = values.astype(F32)

    def backward(u):
        each(4, lambda r: branch_back(u, r))
        send_messages(cm, TO_OWNER, dprod_send, dprod_recv, u, D_PRODUCTS, 1)
        if u == 1:
            put_early(5, out_part(1))
            put_early(4, proj_part(1, 4))
        else:
            for g in range(4):
                put_early(g, proj_part(1, g))
            put_early(6, proj_part(0, 4))
            put_early(7, out_part(0))
            begin_sum(early, EARLY)
        take_messages(dprod_recv, BY_CHANNEL, u, D_PRODUCTS, store_out, 1)
        each(4, lambda h: multiply_back(u, h))
        send_messages(own_out, BY_SOURCE, dedge_send, dedge_recv, u, D_EDGES, 2)
        if u == 0:
            sum_line(early, EARLY)
        take_messages(dedge_recv, FROM_OWNER, u, D_EDGES, store_cm(2), 2)
        each(4, lambda r: edges_back(u, r))
        if u == 1:
            each(4, lambda r: norm_back(1, r))

    def finish():
        for g in range(4):
            values = proj_part(0, g)
            late[0][8 * g : 8 * (g + 1)] = values.reshape(8, 16, 128)
        begin_sum(late, LATE)
        for r in range(4):
            norm_back(0, r)
            if r < 2:
                send_grad(r)
        share_sum(early, EARLY)
        sum_line(late, LATE)
        send_grad(2)
        send_grad(3)
        end_early()
        share_sum(late, LATE)
        end_late()

    loads = [
        pltpu.make_async_copy(source, target, sems.at[LOADS + k])
        for k, (source, target) in enumerate(
            (
                (w_in, w_ref),
                (bias_in, bias_ref),
                (gain_in, gain_ref),
                (shift_in, shift_ref),
                (wo_in, wo_ref),
                (ob_in, ob_ref),
            )
        )
    ]
    for load in loads:
        load.start()
    pl.semaphore_wait(barrier, jnp.where(away, 48, 46))

    move(mask_in, mask_ref, MASK_MOVE, MASK_MOVE + 1, worker)
    for r in range(4):
        move(pair_in.at[r], pair_buf.at[r], PAIR_SENT, PAIR_CAME + r, worker)
    for load in loads:
        load.wait()
    prepare()
    prepare_update(0)
    prepare_update(1)
    wait_bytes(mask_ref, MASK_MOVE + 1)
    forward(0)
    forward(1)
    backward(1)
    backward(0)
    finish()
    wait_bytes(grad_buf, GRAD_CAME)
    grad_ref[...] = grad_buf[...]

    @pl.when(away)
    def _():
        wait_bytes(pair_buf, PAIR_SENT)
        wait_bytes(mask_ref, MASK_MOVE)
        wait_bytes(cot_buf, COT_MOVE)
        wait_bytes(grad_buf, GRAD_SENT)

    for step, sent in (
        (EDGES, edge_send),
        (PRODUCTS, prod_send),
        (D_PRODUCTS, dprod_send),
        (D_EDGES, dedge_send),
    ):
        for u in range(2):
            wait_bytes(sent.at[u, pl.ds(0, 31)], step + u)
    sums_sent(early, EARLY)
    sums_sent(late, LATE)


def shards(
    pair_repr,
    pair_mask,
    cotangent,
    proj_weight,
    proj_bias,
    norm_gain,
    norm_shift,
    out_weight,
    out_bias,
):
    def real(*shape):
        return pltpu.VMEM(shape, F32)

    def half(*shape):
        return pltpu.VMEM(shape, BF16)

    vmem = pl.BlockSpec(memory_space=pltpu.VMEM)
    pair_grad, proj_grad, out_grad = pl.pallas_call(
        kernel,
        out_shape=(
            jax.ShapeDtypeStruct((4, 128, 128), BF16),
            jax.ShapeDtypeStruct((2, 128, 640), F32),
            jax.ShapeDtypeStruct((2, 128, 128), F32),
        ),
        in_specs=[pl.BlockSpec(memory_space=pl.ANY)] * 9,
        out_specs=(vmem, vmem, vmem),
        scratch_shapes=[
            half(2, 128, 640),
            real(2, 640),
            real(2, 256),
            real(2, 256),
            half(2, 128, 128),
            real(2, 128),
            pltpu.VMEM((4, 128), jnp.int32),
            half(4, 128, 128),
            half(4, 128, 128),
            half(4, 128, 128),
            half(4, 128, 128),
            half(2, 640, 128),
            half(2, 128, 128),
            half(4, 128, 128),
            real(2, 10, 128, 128),
            real(2, 4, 128, 128),
            half(2, 4, 128, 128),
            real(2, 4, 128, 128),
            real(2, 4, 1, 128),
            real(2, 4, 4, 128, 128),
            real(2, 4, 128, 128),
            real(2, 4, 128, 128),
            real(2, 4, 128, 128),
            real(2, 4, 1, 128),
            half(2, 4, 128, 128),
            real(4, 128, 128),
            half(4, 640, 128),
            half(4, 128, 128),
            half(4, 128, 256),
            half(2, 4, 128, 256),
            half(4, 128, 256),
            half(2, 32, 32, 128),
            half(2, 32, 32, 128),
            half(2, 32, 16, 128),
            half(2, 32, 16, 128),
            half(2, 32, 16, 128),
            half(2, 32, 16, 128),
            half(2, 32, 32, 128),
            half(2, 32, 32, 128),
            half(32, 32, 128),
            half(32, 32, 128),
            half(32, 128),
            half(16, 32, 128),
            half(32, 128),
            half(32, 32, 128),
            half(32, 16, 128),
            half(32, 16, 128),
            half(16, 128),
            half(16, 16, 128),
            half(16, 128),
            half(32, 16, 128),
            pltpu.SemaphoreType.DMA((SEMAPHORES,)),
        ],
        compiler_params=pltpu.CompilerParams(
            collective_id=1, has_side_effects=True, vmem_limit_bytes=63 << 20
        ),
    )(
        pair_repr[0],
        pair_mask[0],
        cotangent[0],
        proj_weight,
        proj_bias,
        norm_gain,
        norm_shift,
        out_weight,
        out_bias,
    )
    return pair_grad[None], proj_grad, out_grad


def solution(mesh):
    placed = (
        P("dp", "dap", None, None),
        P("dp", "dap", None),
        P("dp", "dap", None, None),
        P(),
        P(),
        P(),
        P(),
        P(),
        P(),
    )
    return jax.shard_map(
        shards,
        mesh=mesh,
        in_specs=placed,
        out_specs=(P("dp", "dap", None, None), P(), P()),
        check_vma=False,
    )
```

```python
import jax
import jax.numpy as jnp
from jax import lax
from jax.experimental import pallas as pl
from jax.experimental.pallas import tpu as pltpu
from jax.sharding import PartitionSpec as P

NORM_EPSILON = 1e-05
MESH = pl.DeviceIdType.MESH
F32 = jnp.float32
BF16 = jnp.bfloat16
EDGES, PRODUCTS, D_PRODUCTS, D_EDGES = 0, 2, 4, 6
GAIN_IN, SHIFT_IN, GAIN_OUT, SHIFT_OUT, OUT_BIAS = 5, 6, 7, 8, 9
TO_OWNER, FROM_OWNER, BY_CHANNEL, BY_SOURCE = 0, 1, 2, 3
RECEIVED, EARLY, LATE, LOADS, PAIR_SENT, PAIR_CAME = 8, 40, 46, 52, 58, 59
MASK_MOVE, COT_MOVE, GRAD_SENT, GRAD_CAME, SEMAPHORES = 63, 65, 67, 68, 69
FAR_FIRST = (2, 3, 1, 0)


def dot(a, b):
    return jnp.dot(a, b, preferred_element_type=F32)


def dot_nt(a, b):
    return lax.dot_general(a, b, (((1,), (1,)), ((), ())), preferred_element_type=F32)


def transposed(a):
    return a.astype(F32).T.astype(BF16)


def sigmoid(a):
    return 0.5 * jnp.tanh(0.5 * a) + 0.5


def channel_mean(a):
    return jnp.sum(a, axis=0, keepdims=True) * (1.0 / a.shape[0])


def normalise(values):
    centred = values - channel_mean(values)
    scale = lax.rsqrt(channel_mean(centred * centred) + NORM_EPSILON)
    return centred * scale, scale


def norm_pullback(unit, scale, d_unit):
    return scale * (d_unit - channel_mean(d_unit) - unit * channel_mean(d_unit * unit))


def each(count, body):
    for step in range(count):
        body(step)


def kernel(
    pair_in,
    mask_in,
    cot_in,
    w_in,
    bias_in,
    gain_in,
    shift_in,
    wo_in,
    ob_in,
    grad_ref,
    proj_ref,
    out_ref,
    w_ref,
    bias_ref,
    gain_ref,
    shift_ref,
    wo_ref,
    ob_ref,
    mask_ref,
    pair_buf,
    cot_buf,
    grad_send,
    grad_buf,
    w_t,
    wo_t,
    perm,
    col,
    state,
    normed,
    unit_in,
    scale_in,
    edge,
    gate,
    branch,
    unit_out,
    scale_out,
    mixed,
    up,
    d_edge,
    d_branch,
    cm,
    own,
    own_out,
    edge_send,
    edge_recv,
    prod_send,
    prod_recv,
    dprod_send,
    dprod_recv,
    dedge_send,
    dedge_recv,
    early_part,
    early_planes,
    early_own,
    early_lines,
    early_sum,
    early_totals,
    late_part,
    late_planes,
    late_own,
    late_lines,
    late_sum,
    late_totals,
    sems,
):
    early = (early_part, early_planes, early_own, early_lines, early_sum, early_totals)
    late = (late_part, late_planes, late_own, late_lines, late_sum, late_totals)
    dp = lax.axis_index("dp")
    dap = lax.axis_index("dap")
    core, z_hi, x = dp & 1, (dp >> 1) & 1, dp >> 2
    y, z_lo = dap >> 3, dap & 7
    home_x = z_lo & 3
    member = y * 8 + core * 4 + x
    slot = y * 8 + core * 4 + ((x + 4 - home_x) & 3)
    z = z_hi * 8 + z_lo

    def member_device(k):
        return ((k & 3) * 4 + z_hi * 2 + ((k >> 2) & 1), (k >> 3) * 8 + z_lo)

    def slot_device(k):
        return (((k + home_x) & 3) * 4 + z_hi * 2 + ((k >> 2) & 1), (k >> 3) * 8 + z_lo)

    def line_device(k):
        return (x * 4 + (k >> 3) * 2 + core, y * 8 + (k & 7))

    worker = (((z_lo + x) & 3) * 4 + z_hi * 2 + (z_lo >> 2), y * 8 + core * 4 + x)
    home = (
        home_x * 4 + z_hi * 2 + (z_lo >> 2),
        slot,
    )
    away = (worker[0] != dp) | (worker[1] != dap)

    barrier = pltpu.get_barrier_semaphore()

    def greet(device, own_index, count):
        @pl.loop(1, count)
        def _(k):
            pl.semaphore_signal(
                barrier, inc=1, device_id=device((own_index + k) & (count - 1)), device_id_type=MESH
            )

    @pl.when(away)
    def _():
        pl.semaphore_signal(barrier, inc=1, device_id=worker, device_id_type=MESH)
        pl.semaphore_signal(barrier, inc=1, device_id=home, device_id_type=MESH)

    greet(member_device, member, 32)
    greet(line_device, z, 16)

    def send(source, target, sent, received, device):
        pltpu.make_async_remote_copy(
            src_ref=source,
            dst_ref=target,
            send_sem=sems.at[sent],
            recv_sem=sems.at[received],
            device_id=device,
            device_id_type=MESH,
        ).start()

    def wait_bytes(ref, semaphore):
        pltpu.make_async_copy(ref, ref, sems.at[semaphore]).wait()

    def far_first(k):
        order = 32 - k
        x_rank, y_rank = (order >> 1) & 3, order >> 3
        return (x_rank ^ (x_rank >> 1)) | ((order & 1) << 2) | ((y_rank ^ (y_rank >> 1)) << 3)

    def exchange_group(source, landing, u, step, apart):
        group = y ^ apart
        received = RECEIVED + 4 * (step + u) + y

        @pl.loop(0, 7 if apart == 0 else 8)
        def _(k):
            order = 7 - k
            x_rank = order >> 1
            offset = (x_rank ^ (x_rank >> 1)) | ((order & 1) << 2)
            d = group * 8 + ((slot & 7) ^ offset)
            send(
                source.at[u, d], landing.at[u, slot], step + u, received, slot_device(d)
            )

        if apart == 0:
            pltpu.make_async_copy(
                source.at[u, slot], landing.at[u, slot], sems.at[received]
            ).start()

    def move(source, target, sent, came, device):
        @pl.when(away)
        def _():
            pltpu.make_async_remote_copy(
                src_ref=source,
                dst_ref=target,
                send_sem=sems.at[sent],
                recv_sem=sems.at[came],
                device_id=device,
                device_id_type=MESH,
            ).start()

        @pl.when(jnp.logical_not(away))
        def _():
            pltpu.make_async_copy(source, target, sems.at[came]).start()

    def prepare():
        row = lax.broadcasted_iota(jnp.int32, (128, 128), 0)
        lane = lax.broadcasted_iota(jnp.int32, (128, 128), 1)
        by_device = (row & 3) * 32 + (row >> 4) * 4 + ((row >> 2) & 3)
        by_device_t = (lane & 3) * 32 + (lane >> 4) * 4 + ((lane >> 2) & 3)
        by_channel = ((row >> 2) & 7) * 16 + (row >> 5) * 4 + (row & 3)
        by_channel_t = ((lane >> 2) & 7) * 16 + (lane >> 5) * 4 + (lane & 3)
        perm[TO_OWNER] = jnp.where(lane == by_device, 1.0, 0.0).astype(BF16)
        perm[FROM_OWNER] = jnp.where(row == by_device_t, 1.0, 0.0).astype(BF16)
        perm[BY_CHANNEL] = jnp.where(lane == by_channel, 1.0, 0.0).astype(BF16)
        perm[BY_SOURCE] = jnp.where(row == by_channel_t, 1.0, 0.0).astype(BF16)

    def prepare_update(u):
        rows = [bias_ref[u : u + 1, 128 * g : 128 * (g + 1)] for g in range(5)]
        rows += [gain_ref[u : u + 1, 0:128], shift_ref[u : u + 1, 0:128]]
        rows += [gain_ref[u : u + 1, 128:256], shift_ref[u : u + 1, 128:256]]
        rows += [ob_ref[u : u + 1, :]]
        for k, values in enumerate(rows):
            col[u, k] = jnp.broadcast_to(values, (128, 128)).T
        for g in range(5):
            block = slice(128 * g, 128 * (g + 1))
            w_t[u, block, :] = transposed(w_ref[u, :, block])
        wo_t[u] = transposed(wo_ref[u])

    def project(u, r):
        unit, scale = normalise(state[u, r])
        values = (unit * col[u, GAIN_IN] + col[u, SHIFT_IN]).astype(BF16)
        unit_in[u, r] = unit
        scale_in[u, r] = scale
        normed[u, r] = values
        keep = mask_ref[pl.ds(r, 1), :].astype(F32)
        for side in range(2):
            g = 2 * side
            pre = dot(w_t[u, 128 * g : 128 * (g + 2), :], values)
            linear = pre[:128] + col[u, g]
            opened = sigmoid(pre[128:] + col[u, g + 1])
            edge[u, r, g] = linear
            edge[u, r, g + 1] = opened
            cm[r, :, 128 * side : 128 * (side + 1)] = (opened * linear * keep).astype(BF16)

    def open_gate(u, r):
        gate[u, r] = sigmoid(dot(w_t[u, 512:640, :], normed[u, r]) + col[u, 4])

    def pack(target, u, block, values, width):
        for side in range(width):
            target[u, block, 16 * side : 16 * (side + 1), :] = values[
                :, 128 * side : 128 * (side + 1)
            ].reshape(8, 16, 128)

    def unpack(landing, u, block, width):
        sides = [
            landing[u, block, 16 * side : 16 * (side + 1), :].reshape(128, 128)
            for side in range(width)
        ]
        return sides[0] if width == 1 else jnp.concatenate(sides, axis=1)

    def group_slices(apart):
        group = y ^ apart
        return (
            pl.ds(pl.multiple_of(group * 8, 8), 8),
            pl.ds(pl.multiple_of(group * 32, 32), 32),
        )

    def send_messages(source, which, target, landing, u, step, width):
        for apart in FAR_FIRST:
            block, rows = group_slices(apart)
            values = jnp.concatenate(
                [source[q, rows, 0 : 128 * width] for q in range(4)], axis=0
            )
            pack(target, u, block, dot(perm[which], values).astype(BF16), width)
            exchange_group(target, landing, u, step, apart)

    def take_messages(landing, which, u, step, target, width):
        for apart in FAR_FIRST:
            block, rows = group_slices(apart)
            wait_bytes(landing.at[u, block], RECEIVED + 4 * (step + u) + (y ^ apart))
            values = dot(perm[which], unpack(landing, u, block, width)).astype(BF16)
            for q in range(4):
                target(q, rows, values[32 * q : 32 * (q + 1)])

    def store_own(u):
        def store(q, rows, values):
            own[u, q, rows, :] = values

        return store

    def store_out(q, rows, values):
        own_out[q, rows, 0:128] = values

    def store_cm(width):
        def store(q, rows, values):
            cm[q, rows, 0 : 128 * width] = values

        return store

    def multiply(u, h):
        left, right = own[u, h, :, 0:128], own[u, h, :, 128:256]
        if u == 0:
            values = dot_nt(left, right)
        else:
            values = dot(transposed(left), right)
        own_out[h, :, 0:128] = values.astype(BF16)

    def multiply_back(u, h):
        left, right = own[u, h, :, 0:128], own[u, h, :, 128:256]
        d_product = own_out[h, :, 0:128]
        if u == 0:
            d_left = dot(d_product, right)
            d_right = dot(transposed(d_product), left)
        else:
            d_left = dot_nt(right, d_product)
            d_right = dot(left, d_product)
        own_out[h, :, 0:128] = d_left.astype(BF16)
        own_out[h, :, 128:256] = d_right.astype(BF16)

    def mix(u, r):
        unit, scale = normalise(cm[r, :, 0:128].astype(F32))
        values = (unit * col[u, GAIN_OUT] + col[u, SHIFT_OUT]).astype(BF16)
        unit_out[u, r] = unit
        scale_out[u, r] = scale
        mixed[u, r] = values
        result = dot(wo_t[u], values) + col[u, OUT_BIAS]
        branch[u, r] = result
        if u == 0:
            state[1, r] = (state[0, r] + gate[0, r] * result).astype(BF16).astype(F32)

    def forward(u):
        if u == 0:
            for r in range(4):
                wait_bytes(pair_buf.at[r], PAIR_CAME + r)
                state[0, r] = pair_buf[r].astype(F32).T
                project(0, r)
        else:
            each(4, lambda r: project(u, r))
        send_messages(cm, TO_OWNER, edge_send, edge_recv, u, EDGES, 2)
        each(4, lambda r: open_gate(u, r))
        if u == 0:
            move(cot_in, cot_buf, COT_MOVE, COT_MOVE + 1, worker)
        else:
            wait_bytes(cot_buf, COT_MOVE + 1)

            def load_cotangent(r):
                up[r] = cot_buf[r].astype(F32).T

            each(4, load_cotangent)
        take_messages(edge_recv, BY_CHANNEL, u, EDGES, store_own(u), 2)
        each(4, lambda h: multiply(u, h))
        send_messages(own_out, BY_SOURCE, prod_send, prod_recv, u, PRODUCTS, 1)
        take_messages(prod_recv, FROM_OWNER, u, PRODUCTS, store_cm(1), 1)
        each(4, lambda r: mix(u, r))

    def branch_back(u, r):
        opened = gate[u, r]
        through = up[r] * opened
        values = through.astype(BF16)
        d_branch[r] = values
        d_edge[r, 512:640, :] = (through * branch[u, r] * (1.0 - opened)).astype(BF16)
        d_unit = dot(wo_ref[u], values) * col[u, GAIN_OUT]
        cm[r, :, 0:128] = norm_pullback(unit_out[u, r], scale_out[u, r], d_unit).astype(BF16)

    def edges_back(u, r):
        keep = mask_ref[pl.ds(r, 1), :].astype(F32)
        for side in range(2):
            g = 2 * side
            linear, opened = edge[u, r, g], edge[u, r, g + 1]
            through = cm[r, :, 128 * side : 128 * (side + 1)].astype(F32) * keep * opened
            d_edge[r, 128 * g : 128 * (g + 1), :] = through.astype(BF16)
            d_edge[r, 128 * (g + 1) : 128 * (g + 2), :] = (
                through * linear * (1.0 - opened)
            ).astype(BF16)

    def norm_back(u, r):
        d_unit = dot(w_ref[u], d_edge[r]) * col[u, GAIN_IN]
        result = up[r] + norm_pullback(unit_in[u, r], scale_in[u, r], d_unit)
        if u == 1:
            up[r] = result
        else:
            grad_send[r] = result.T.astype(BF16)

    def send_grad(r):
        move(grad_send.at[r], grad_buf.at[r], GRAD_SENT, GRAD_CAME, home)

    def proj_part(u, g):
        total = dot_nt(normed[u, 0], d_edge[0, 128 * g : 128 * (g + 1), :])
        for r in range(1, 4):
            total += dot_nt(normed[u, r], d_edge[r, 128 * g : 128 * (g + 1), :])
        return total.astype(BF16)

    def out_part(u):
        total = dot_nt(mixed[u, 0], d_branch[0])
        for r in range(1, 4):
            total += dot_nt(mixed[u, r], d_branch[r])
        return total.astype(BF16)

    def begin_sum(unit, step):
        part, planes = unit[0], unit[1]

        @pl.loop(1, 32)
        def _(k):
            j = member ^ far_first(k)
            send(part.at[j], planes.at[member], step, step + 1, member_device(j))

        pltpu.make_async_copy(part.at[member], planes.at[member], sems.at[step + 1]).start()

    def sum_line(unit, step):
        planes, own_part, lines = unit[1], unit[2], unit[3]
        wait_bytes(planes, step + 1)
        own_part[...] = jnp.sum(planes[...].astype(F32), axis=0).astype(BF16)

        @pl.loop(1, 16)
        def _(k):
            send(own_part, lines.at[z], step + 2, step + 3, line_device(z ^ k))

        pltpu.make_async_copy(own_part, lines.at[z], sems.at[step + 3]).start()

    def share_sum(unit, step):
        lines, own_total, totals = unit[3], unit[4], unit[5]
        wait_bytes(lines, step + 3)
        own_total[...] = jnp.sum(lines[...].astype(F32), axis=0).astype(BF16)

        @pl.loop(1, 32)
        def _(k):
            send(
                own_total,
                totals.at[member],
                step + 4,
                step + 5,
                member_device(member ^ far_first(k)),
            )

        pltpu.make_async_copy(own_total, totals.at[member], sems.at[step + 5]).start()

    def sums_sent(unit, step):
        planes, lines, totals = unit[1], unit[3], unit[5]
        wait_bytes(planes.at[pl.ds(0, 31)], step)
        wait_bytes(lines.at[pl.ds(0, 15)], step + 2)
        wait_bytes(totals.at[pl.ds(0, 31)], step + 4)

    def put_early(block, values):
        early[0][4 * block : 4 * (block + 1)] = values.reshape(4, 32, 128)

    def end_early():
        wait_bytes(early[5], EARLY + 5)
        targets = [proj_ref.at[1, :, pl.ds(128 * g, 128)] for g in range(5)]
        targets += [out_ref.at[1], proj_ref.at[0, :, pl.ds(512, 128)], out_ref.at[0]]
        for block, target in enumerate(targets):
            values = early[5][4 * block : 4 * (block + 1)]
            target[...] = values.reshape(128, 128)

    def end_late():
        wait_bytes(late[5], LATE + 5)
        for g in range(4):
            values = late[5][8 * g : 8 * (g + 1)].reshape(128, 128)
            proj_ref[0, :, 128 * g : 128 * (g + 1)] = values

    def backward(u):
        each(4, lambda r: branch_back(u, r))
        send_messages(cm, TO_OWNER, dprod_send, dprod_recv, u, D_PRODUCTS, 1)
        if u == 1:
            put_early(5, out_part(1))
            put_early(4, proj_part(1, 4))
        else:
            for g in range(4):
                put_early(g, proj_part(1, g))
            put_early(6, proj_part(0, 4))
            put_early(7, out_part(0))
            begin_sum(early, EARLY)
        take_messages(dprod_recv, BY_CHANNEL, u, D_PRODUCTS, store_out, 1)
        each(4, lambda h: multiply_back(u, h))
        send_messages(own_out, BY_SOURCE, dedge_send, dedge_recv, u, D_EDGES, 2)
        if u == 0:
            sum_line(early, EARLY)
        take_messages(dedge_recv, FROM_OWNER, u, D_EDGES, store_cm(2), 2)
        each(4, lambda r: edges_back(u, r))
        if u == 1:
            each(4, lambda r: norm_back(1, r))

    def finish():
        for g in range(4):
            values = proj_part(0, g)
            late[0][8 * g : 8 * (g + 1)] = values.reshape(8, 16, 128)
        begin_sum(late, LATE)
        for r in range(4):
            norm_back(0, r)
            if r < 2:
                send_grad(r)
        sum_line(late, LATE)
        share_sum(early, EARLY)
        send_grad(2)
        send_grad(3)
        end_early()
        share_sum(late, LATE)
        end_late()

    loads = [
        pltpu.make_async_copy(source, target, sems.at[LOADS + k])
        for k, (source, target) in enumerate(
            (
                (w_in, w_ref),
                (bias_in, bias_ref),
                (gain_in, gain_ref),
                (shift_in, shift_ref),
                (wo_in, wo_ref),
                (ob_in, ob_ref),
            )
        )
    ]
    for load in loads:
        load.start()
    pl.semaphore_wait(barrier, jnp.where(away, 48, 46))

    move(mask_in, mask_ref, MASK_MOVE, MASK_MOVE + 1, worker)
    for r in range(4):
        move(pair_in.at[r], pair_buf.at[r], PAIR_SENT, PAIR_CAME + r, worker)
    for load in loads:
        load.wait()
    prepare()
    prepare_update(0)
    prepare_update(1)
    wait_bytes(mask_ref, MASK_MOVE + 1)
    forward(0)
    forward(1)
    backward(1)
    backward(0)
    finish()
    wait_bytes(grad_buf, GRAD_CAME)
    grad_ref[...] = grad_buf[...]

    @pl.when(away)
    def _():
        wait_bytes(pair_buf, PAIR_SENT)
        wait_bytes(mask_ref, MASK_MOVE)
        wait_bytes(cot_buf, COT_MOVE)
        wait_bytes(grad_buf, GRAD_SENT)

    for step, sent in (
        (EDGES, edge_send),
        (PRODUCTS, prod_send),
        (D_PRODUCTS, dprod_send),
        (D_EDGES, dedge_send),
    ):
        for u in range(2):
            wait_bytes(sent.at[u, pl.ds(0, 31)], step + u)
    sums_sent(early, EARLY)
    sums_sent(late, LATE)


def widen_kernel(grad_in, proj_in, out_in, grad_ref, proj_ref, out_ref):
    grad_ref[...] = grad_in[...]
    proj_ref[...] = proj_in[...].astype(F32)
    out_ref[...] = out_in[...].astype(F32)


def shards(
    pair_repr,
    pair_mask,
    cotangent,
    proj_weight,
    proj_bias,
    norm_gain,
    norm_shift,
    out_weight,
    out_bias,
):
    def real(*shape):
        return pltpu.VMEM(shape, F32)

    def half(*shape):
        return pltpu.VMEM(shape, BF16)

    vmem = pl.BlockSpec(memory_space=pltpu.VMEM)
    pair_grad, proj_grad, out_grad = pl.pallas_call(
        kernel,
        out_shape=(
            jax.ShapeDtypeStruct((4, 128, 128), BF16),
            jax.ShapeDtypeStruct((2, 128, 640), BF16),
            jax.ShapeDtypeStruct((2, 128, 128), BF16),
        ),
        in_specs=[pl.BlockSpec(memory_space=pl.ANY)] * 9,
        out_specs=(vmem, vmem, vmem),
        scratch_shapes=[
            half(2, 128, 640),
            real(2, 640),
            real(2, 256),
            real(2, 256),
            half(2, 128, 128),
            real(2, 128),
            pltpu.VMEM((4, 128), jnp.int32),
            half(4, 128, 128),
            half(4, 128, 128),
            half(4, 128, 128),
            half(4, 128, 128),
            half(2, 640, 128),
            half(2, 128, 128),
            half(4, 128, 128),
            real(2, 10, 128, 128),
            real(2, 4, 128, 128),
            half(2, 4, 128, 128),
            real(2, 4, 128, 128),
            real(2, 4, 1, 128),
            real(2, 4, 4, 128, 128),
            real(2, 4, 128, 128),
            real(2, 4, 128, 128),
            real(2, 4, 128, 128),
            real(2, 4, 1, 128),
            half(2, 4, 128, 128),
            real(4, 128, 128),
            half(4, 640, 128),
            half(4, 128, 128),
            half(4, 128, 256),
            half(2, 4, 128, 256),
            half(4, 128, 256),
            half(2, 32, 32, 128),
            half(2, 32, 32, 128),
            half(2, 32, 16, 128),
            half(2, 32, 16, 128),
            half(2, 32, 16, 128),
            half(2, 32, 16, 128),
            half(2, 32, 32, 128),
            half(2, 32, 32, 128),
            half(32, 32, 128),
            half(32, 32, 128),
            half(32, 128),
            half(16, 32, 128),
            half(32, 128),
            half(32, 32, 128),
            half(32, 16, 128),
            half(32, 16, 128),
            half(16, 128),
            half(16, 16, 128),
            half(16, 128),
            half(32, 16, 128),
            pltpu.SemaphoreType.DMA((SEMAPHORES,)),
        ],
        compiler_params=pltpu.CompilerParams(
            collective_id=1, has_side_effects=True, vmem_limit_bytes=63 << 20
        ),
    )(
        pair_repr[0],
        pair_mask[0],
        cotangent[0],
        proj_weight,
        proj_bias,
        norm_gain,
        norm_shift,
        out_weight,
        out_bias,
    )
    pair_grad, proj_grad, out_grad = pl.pallas_call(
        widen_kernel,
        out_shape=(
            jax.ShapeDtypeStruct((4, 128, 128), BF16),
            jax.ShapeDtypeStruct((2, 128, 640), F32),
            jax.ShapeDtypeStruct((2, 128, 128), F32),
        ),
        in_specs=[vmem] * 3,
        out_specs=(vmem,) * 3,
        compiler_params=pltpu.CompilerParams(vmem_limit_bytes=63 << 20),
    )(pair_grad, proj_grad, out_grad)
    return pair_grad[None], proj_grad, out_grad


def solution(mesh):
    placed = (
        P("dp", "dap", None, None),
        P("dp", "dap", None),
        P("dp", "dap", None, None),
        P(),
        P(),
        P(),
        P(),
        P(),
        P(),
    )
    return jax.shard_map(
        shards,
        mesh=mesh,
        in_specs=placed,
        out_specs=(P("dp", "dap", None, None), P(), P()),
        check_vma=False,
    )
```
